768 devices in a mesh: fsdp: 24 (over z, core), rep: 32 (over x, y).
Axes of the slice: x: 4, y: 8, z: 12, core: 2. Of those that a mesh axis runs over, the one named last changes fastest.
Arguments:
- grad_partial: bfloat16 [32, 144, 512, 512], P('rep', 'fsdp'), may hold values from -3 to 3
- basis_left: bfloat16 [144, 512, 512], P('fsdp'), may hold values from -0.25 to 0.25
- basis_right: bfloat16 [144, 512, 512], P('fsdp'), may hold values from -0.25 to 0.25
- owner_table: int32 [144], replicated, may hold values from 0 to 23, as said below
- moment_first: bfloat16 [24, 12, 512, 512], P('fsdp', None, 'rep'), may hold values from -6 to 6
- moment_second: float32 [24, 12, 512, 512], P('fsdp', None, 'rep'), may hold values from 0.1 to 10
Outputs:
- update: bfloat16 [144, 512, 512], P('fsdp', 'rep')
- new_first: bfloat16 [24, 12, 512, 512], P('fsdp', None, 'rep')
- new_second: float32 [24, 12, 512, 512], P('fsdp', None, 'rep')
The draws below stay inside these ranges and needn't reach their ends.
Inputs may be any that keep to these rules, and one draw needn't show every extreme that they name: `owner_table`: block b belongs to the shard of fsdp index b // 6. At most 1 block of one shard name the same owner, and at most 12 blocks in all name the same owner; both bounds are reached in every draw.
All inputs are finite; a program needn't handle non-finite values.
Results may differ from the reference program's by a relative error of at most 0.015.
Values may be sent and summed in bfloat16 or wider, within the bound.
A program may use at most 64 MiB of HBM per device.

```python
import math
import jax
import jax.numpy as jnp
from jax import lax

BLOCK = 512
SHARD_BLOCKS = 6
BLOCKS = 144
OWNER_SLOTS = 12
N_FSDP = 24
N_REP = 32


def draw_owner_table(key, part):
    key = jax.random.fold_in(key, 7)
    key_owner, key_block, key_shard = jax.random.split(key, 3)
    owner_perm = jax.random.permutation(key_owner, N_FSDP)
    block_perm = jax.random.permutation(key_block, SHARD_BLOCKS)
    shard_perm = jax.random.permutation(key_shard, N_FSDP)
    position = jnp.arange(N_FSDP * SHARD_BLOCKS, dtype=jnp.int32)
    source = position // SHARD_BLOCKS
    local = position % SHARD_BLOCKS
    sequence = block_perm[local] * N_FSDP + shard_perm[source]
    hot_count = N_FSDP // 4
    hot_span = hot_count * 2 * SHARD_BLOCKS
    heavy = sequence // (2 * SHARD_BLOCKS)
    light = hot_count + (sequence - hot_span) // (2 * SHARD_BLOCKS // 3)
    owner_rank = jnp.where(sequence < hot_span, heavy, light)
    return owner_perm[owner_rank].astype(jnp.int32)


def shard_levels(stream_key, dims, cuts, smallest, largest):
    def one(dim, blocks):
        draws = jax.random.uniform(jax.random.fold_in(jax.random.fold_in(stream_key, 6), dim), (blocks,), jnp.float32, smallest / len(cuts), largest / len(cuts))
        return jnp.repeat(jnp.exp(draws), dims[dim] // blocks).reshape((-1,) + (1,) * (len(dims) - dim - 1))

    level = one(*cuts[0])
    for cut in cuts[1:]:
        level = level * one(*cut)
    return level


def noise(key, dims, deviation, bound, shards=(), kind=jnp.bfloat16):
    drawn = jax.random.normal(key, dims, jnp.float32) * deviation
    if len(shards) > 0:
        drawn = shard_levels(key, dims, shards, -0.22, 0.18) * drawn
    return jnp.clip(drawn, min=-bound, max=bound).astype(kind)


def setup_inputs(seed: int = 0) -> dict:
    key_of = jax.random.split(jax.random.key(seed), 7)
    return {
        "grad_partial": noise(key_of[0], (N_REP, BLOCKS, BLOCK, BLOCK), 0.2, 3.0, ((0, 32), (1, 24))),
        "basis_left": noise(key_of[1], (BLOCKS, BLOCK, BLOCK), BLOCK ** -0.5, 0.25, ((0, 24),)),
        "basis_right": noise(key_of[2], (BLOCKS, BLOCK, BLOCK), BLOCK ** -0.5, 0.25, ((0, 24),)),
        "owner_table": draw_owner_table(jax.random.fold_in(key_of[6], 71), 0),
        "moment_first": noise(key_of[4], (N_FSDP, OWNER_SLOTS, BLOCK, BLOCK), 1.0, 6.0, ((0, 24), (2, 32))),
        "moment_second": jnp.clip(jnp.exp(math.log(10.0) - 4.6051702 * jax.random.uniform(key_of[5], (N_FSDP, OWNER_SLOTS, BLOCK, BLOCK), jnp.float32) ** shard_levels(key_of[5], (N_FSDP, OWNER_SLOTS, BLOCK, BLOCK), ((0, 24), (2, 32)), -0.2, 0.2)), 0.1, 10.0),
    }


BETA_ONE = 0.9
BETA_TWO = 0.95
EPSILON = 1e-08

def rounded(values):
    return lax.optimization_barrier(values.astype(jnp.bfloat16)).astype(jnp.float32)

def block_slots(owner_table):
    position = jnp.arange(owner_table.shape[0], dtype=jnp.int32)
    same_owner = owner_table[:, None] == owner_table[None, :]
    earlier = position[None, :] < position[:, None]
    return lax.optimization_barrier(jnp.sum((same_owner & earlier).astype(jnp.int32), axis=1)).astype(jnp.int32)

def reference(grad_partial, basis_left, basis_right, owner_table, moment_first, moment_second):

    def rotate_block(position):
        partial_block = lax.dynamic_index_in_dim(grad_partial, position, 1, False).astype(jnp.float32)
        left_basis = lax.dynamic_index_in_dim(basis_left, position, 0, False).astype(jnp.float32)
        right_basis = lax.dynamic_index_in_dim(basis_right, position, 0, False).astype(jnp.float32)
        right_part = rounded(jnp.einsum('rij,jl->ril', partial_block, right_basis))
        rotated_part = rounded(jnp.einsum('ji,rjl->ril', left_basis, right_part))
        return lax.optimization_barrier(jnp.sum(rotated_part, axis=0)).astype(jnp.bfloat16)
    rotated_grad = lax.map(rotate_block, jnp.arange(BLOCKS, dtype=jnp.int32))
    owner_rank = block_slots(owner_table)
    first_old = moment_first[owner_table, owner_rank].astype(jnp.float32)
    second_old = moment_second[owner_table, owner_rank]
    gradient = rotated_grad.astype(jnp.float32)
    first_new = BETA_ONE * first_old + (1.0 - BETA_ONE) * gradient
    second_new = BETA_TWO * second_old + (1.0 - BETA_TWO) * gradient * gradient
    direction = (first_new / (jnp.sqrt(second_new) + EPSILON)).astype(jnp.bfloat16)
    new_first = moment_first.at[owner_table, owner_rank].set(first_new.astype(jnp.bfloat16))
    new_second = moment_second.at[owner_table, owner_rank].set(second_new)

    def back_block(position):
        left_basis = lax.dynamic_index_in_dim(basis_left, position, 0, False)
        right_basis = lax.dynamic_index_in_dim(basis_right, position, 0, False)
        direction_block = lax.dynamic_index_in_dim(direction, position, 0, False)
        left_back = jnp.dot(left_basis, direction_block, preferred_element_type=jnp.float32).astype(jnp.bfloat16)
        return jnp.dot(left_back, right_basis.T, preferred_element_type=jnp.float32).astype(jnp.bfloat16)
    update = lax.map(back_block, jnp.arange(BLOCKS, dtype=jnp.int32))
    return (update, new_first, new_second)
```

```python
import functools

import jax
import jax.numpy as jnp
from jax import lax
from jax.experimental import pallas as pl
from jax.experimental.pallas import tpu as pltpu
from jax.sharding import PartitionSpec as P

BETA_ONE = 0.9
BETA_TWO = 0.95
EPSILON = 1e-08
GRID_X = 4
LANES = 128
CHUNKS = 2
F32 = jnp.float32
BF16 = jnp.bfloat16


def kernel(
    sizes,
    grad_hbm,
    left_hbm,
    right_hbm,
    table,
    first_hbm,
    second_hbm,
    update_hbm,
    new_first_hbm,
    new_second_hbm,
    grad,
    left,
    right,
    first,
    second,
    new_first,
    new_second,
    update,
    total_back,
    part,
    ring_a_x,
    ring_a_y,
    ring_b_y,
    ring_b_x,
    reduced,
    outgoing,
    incoming,
    sendback,
    comeback,
    tiles,
    gathered,
    product,
    rows_in,
    slot_table,
    in_sem,
    out_sem,
    ring_send,
    ring_recv,
    swap_send,
    swap_recv,
):
    fsdp, nx, ny, chunks, width, blocks, slots = sizes
    rep = nx * ny
    cols = width // LANES
    half_blocks = blocks // 2
    units = blocks * cols
    shard = lax.axis_index("fsdp")
    replica = lax.axis_index("rep")
    my_x = replica // ny
    my_y = replica % ny

    def at_fsdp(step):
        return {"fsdp": (shard + step) % fsdp}

    def at_rep(step):
        return {"rep": (replica + step) % rep}

    def load(k, which):
        source, target = ((grad_hbm.at[0], grad), (left_hbm, left), (right_hbm, right))[which]
        return pltpu.make_async_copy(source.at[k], target.at[k], in_sem.at[which, k])

    order = [*range(half_blocks, blocks), *range(half_blocks)]
    for k in order:
        for which in (0, 2, 1):
            load(k, which).start()
    load_first = pltpu.make_async_copy(first_hbm.at[0], first, in_sem.at[3, 0])
    load_second = pltpu.make_async_copy(second_hbm.at[0], second, in_sem.at[3, 1])
    load_first.start()
    load_second.start()

    barrier = pltpu.get_barrier_semaphore()

    def greet(axis):
        def body(step, carry):
            pl.semaphore_signal(
                barrier, inc=1, device_id=axis(step), device_id_type=pl.DeviceIdType.MESH
            )
            return carry

        return body

    lax.fori_loop(1, fsdp, greet(at_fsdp), 0)
    lax.fori_loop(1, rep, greet(at_rep), 0)

    def rotate(q, low, high):
        columns = pl.ds(q * width, width)

        def body(k, carry):
            if q == 0:
                for which in (0, 2, 1):
                    load(k, which).wait()
            right_part = jnp.dot(grad[k], right[k, :, columns], preferred_element_type=F32)
            rotated = lax.dot_general(
                left[k],
                right_part.astype(BF16),
                (((0,), (0,)), ((), ())),
                preferred_element_type=F32,
            )
            part[q, k] = rotated.astype(BF16).reshape(nx, ny, 16, width)
            return carry

        lax.fori_loop(low, high, body, 0)

    def remote(source, target, send, recv, device):
        return pltpu.make_async_remote_copy(
            src_ref=source,
            dst_ref=target,
            send_sem=send,
            recv_sem=recv,
            device_id=device,
            device_id_type=pl.DeviceIdType.MESH,
        )

    sent = []

    def ring(count, position, piece, landing, sems, device):
        reach = count // 2
        flying = {}

        def copy(way, step):
            there = (position + way * (reach - step + 1) + count) % count
            side = 0 if way > 0 else 1
            cut = None if step > 1 else side
            return remote(
                piece(there, cut),
                landing(side, step - 1, cut),
                ring_send.at[sems + (side, step - 1)],
                ring_recv.at[sems + (side, step - 1)],
                device(way),
            )

        for step in range(1, reach + 1):
            for way in (1, -1):
                side = 0 if way > 0 else 1
                if step > 1:
                    flying[way].wait_recv()
                    there = (position + way * (reach - step + 1) + count) % count
                    cut = side if step == 2 else None
                    held = piece(there, cut)
                    held[...] = held[...] + landing(side, step - 2, cut)[...]
                flying[way] = copy(way, step)
                flying[way].start()
                sent.append(flying[way])
            yield
        flying[1].wait_recv()
        flying[-1].wait_recv()

    def split(low, count, cut):
        if cut is None:
            return pl.ds(low, count)
        middle = (count + 1) // 2
        return pl.ds(low, middle) if cut == 0 else pl.ds(low + middle, count - middle)

    def along_x(way):
        return {"rep": ((my_x + way + nx) % nx) * ny + my_y}

    def along_y(way):
        return {"rep": my_x * ny + (my_y + way + ny) % ny}

    def total(own, landed):
        return own.astype(F32) + landed[0].astype(F32) + landed[1].astype(F32)

    def sum_a(q):
        mine = pl.ds(0, half_blocks)
        yield from ring(
            nx,
            my_x,
            lambda there, cut: part.at[q, mine, there, split(0, ny, cut)],
            lambda side, step, cut: ring_a_x.at[q, side, step, :, split(0, ny, cut)],
            (q, 0),
            along_x,
        )
        for k in range(half_blocks):
            part[q, k, my_x] = total(
                part[q, k, my_x], [ring_a_x[q, side, nx // 2 - 1, k] for side in (0, 1)]
            ).astype(BF16)
        yield from ring(
            ny,
            my_y,
            lambda there, cut: part.at[q, split(0, half_blocks, cut), my_x, there],
            lambda side, step, cut: ring_a_y.at[q, side, step, split(0, half_blocks, cut)],
            (q, 1),
            along_y,
        )
        for k in range(half_blocks):
            reduced[q, k] = total(
                part[q, k, my_x, my_y], [ring_a_y[q, side, ny // 2 - 1, k] for side in (0, 1)]
            ).astype(BF16)

    def sum_b(q):
        mine = pl.ds(half_blocks, blocks - half_blocks)
        yield from ring(
            ny,
            my_y,
            lambda there, cut: part.at[q, mine, split(0, nx, cut), there],
            lambda side, step, cut: ring_b_y.at[q, side, step, :, split(0, nx, cut)],
            (q, 2),
            along_y,
        )
        for k in range(blocks - half_blocks):
            part[q, half_blocks + k, :, my_y] = total(
                part[q, half_blocks + k, :, my_y],
                [ring_b_y[q, side, ny // 2 - 1, k] for side in (0, 1)],
            ).astype(BF16)
        yield from ring(
            nx,
            my_x,
            lambda there, cut: part.at[
                q, split(half_blocks, blocks - half_blocks, cut), there, my_y
            ],
            lambda side, step, cut: ring_b_x.at[
                q, side, step, split(0, blocks - half_blocks, cut)
            ],
            (q, 3),
            along_x,
        )
        for k in range(blocks - half_blocks):
            reduced[q, half_blocks + k] = total(
                part[q, half_blocks + k, my_x, my_y],
                [ring_b_x[q, side, nx // 2 - 1, k] for side in (0, 1)],
            ).astype(BF16)

    def lookups():
        def of_shard(other, carry):
            rank, picks = carry
            named = jnp.int32(0)
            for k in range(blocks):
                named += (table[other * blocks + k] == shard).astype(jnp.int32)
            slot_table[other] = jnp.minimum(rank, slots - 1)
            away = (shard - other + fsdp) % fsdp
            picks = tuple(
                jnp.where((named > 0) & (rank == j), away, picks[j]) for j in range(slots)
            )
            return rank + named, picks

        count, picks = lax.fori_loop(
            0, fsdp, of_shard, (jnp.int32(0), (jnp.int32(0),) * slots)
        )
        for j in range(slots):
            slot_table[2 * fsdp + j] = picks[j]
        slot_table[2 * fsdp + slots] = count

        def of_owner(owner, carry):
            block = jnp.int32(0)
            for k in range(blocks):
                block = jnp.where(table[shard * blocks + k] == owner, k, block)
            slot_table[fsdp + owner] = block
            return carry

        lax.fori_loop(0, fsdp, of_owner, 0)

    def swap(q, which, source, target):
        def start(step, carry):
            remote(
                source.at[step],
                target.at[step],
                swap_send.at[q, which],
                swap_recv.at[q, which],
                at_fsdp(step),
            ).start()
            return carry

        lax.fori_loop(1, fsdp, start, 0)
        others = pl.ds(1, fsdp - 1)
        whole = remote(
            source.at[others],
            target.at[others],
            swap_send.at[q, which],
            swap_recv.at[q, which],
            at_fsdp(1),
        )
        sent.append(whole)
        return whole

    def to_owners(q):
        def fill(step, carry):
            block = slot_table[fsdp + (shard + step) % fsdp]
            outgoing[q][step] = reduced[q, block]
            return carry

        lax.fori_loop(1, fsdp, fill, 0)
        incoming[q][0] = reduced[q, slot_table[fsdp + shard]]
        return swap(q, 0, outgoing[q], incoming[q])

    def moments(q, arrival):
        arrival.wait_recv()
        columns = pl.ds(q * width, width)
        count = slot_table[2 * fsdp + slots]

        def body(j, carry):
            gradient = incoming[q][slot_table[2 * fsdp + j]].astype(F32)
            first_old = first[j, :, columns].astype(F32)
            second_old = second[j, :, columns]
            first_now = BETA_ONE * first_old + (1.0 - BETA_ONE) * gradient
            second_now = BETA_TWO * second_old + (1.0 - BETA_TWO) * gradient * gradient
            direction[j] = (first_now / (jnp.sqrt(second_now) + EPSILON)).astype(BF16)
            used = j < count
            new_first[j, :, columns] = jnp.where(used, first_now, first_old).astype(BF16)
            new_second[j, :, columns] = jnp.where(used, second_now, second_old)
            return carry

        direction = tiles[1][q]
        lax.fori_loop(0, slots, body, 0)

        def fill(step, carry):
            sendback[q][step] = direction[slot_table[(shard + step) % fsdp]]
            return carry

        lax.fori_loop(1, fsdp, fill, 0)
        comeback[q][0] = direction[slot_table[shard]]
        return swap(q, 1, sendback[q], comeback[q])

    def to_units(q, arrival):
        arrival.wait_recv()
        piece = tiles[0]
        base = q * units

        for k in range(blocks):
            away = (shard - table[shard * blocks + k] + fsdp) % fsdp
            rows = comeback[q][away]
            for c in range(cols):
                piece[base + k * cols + c] = rows[:, c * LANES : (c + 1) * LANES]

        def start(unit, carry):
            @pl.when(unit != replica)
            def _():
                remote(
                    piece.at[unit],
                    gathered.at[replica],
                    swap_send.at[q, 2],
                    swap_recv.at[q, 2],
                    {"rep": unit},
                ).start()

            @pl.when(unit == replica)
            def _():
                gathered[unit] = piece[unit]

            return carry

        lax.fori_loop(base, base + units, start, 0)

    def unit_copy(q, count):
        return remote(
            gathered.at[pl.ds(0, count)],
            gathered.at[pl.ds(0, count)],
            swap_send.at[q, 2],
            swap_recv.at[q, 2],
            at_rep(1),
        )

    def row_copy(q, count):
        return remote(
            product.at[pl.ds(0, count)],
            product.at[pl.ds(0, count)],
            swap_send.at[q, 3],
            swap_recv.at[q, 3],
            at_rep(1),
        )

    def is_unit(q):
        return (replica >= q * units) & (replica < (q + 1) * units)

    def rotate_left(q):
        @pl.when(is_unit(q))
        def _():
            unit_copy(q, rep - 1).wait_recv()
            block = (replica - q * units) // cols
            back = jnp.dot(
                left[block],
                gathered[...].reshape(rep * 16, LANES),
                preferred_element_type=F32,
            )
            product[...] = back.astype(BF16).reshape(rep, 16, LANES)

            def start(step, carry):
                other = (replica + step) % rep
                remote(
                    product.at[other],
                    rows_in.at[replica],
                    swap_send.at[q, 3],
                    swap_recv.at[q, 3],
                    {"rep": other},
                ).start()
                return carry

            lax.fori_loop(1, rep, start, 0)
            rows_in[replica] = product[replica]

    def finish(q):
        @pl.when(is_unit(q))
        def _():
            row_copy(q, units - 1).wait_recv()

        @pl.when(jnp.logical_not(is_unit(q)))
        def _():
            row_copy(q, units).wait_recv()

        base = q * units
        for k in range(blocks):
            rows = jnp.concatenate([rows_in[base + k * cols + c] for c in range(cols)], axis=1)
            back = lax.dot_general(
                rows,
                right[k, :, q * width : (q + 1) * width],
                (((1,), (1,)), ((), ())),
                preferred_element_type=F32,
            )
            if q > 0:
                back = back + total_back[k]
            if q < chunks - 1:
                total_back[k] = back
            else:
                update[k] = back.astype(BF16)

    lookups()
    arrivals = {}
    started = {}

    def begin(q, after=None):
        rotate(q, half_blocks, blocks)
        if after:
            after()
        b = sum_b(q)
        next(b)
        rotate(q, 0, half_blocks)
        a = sum_a(q)
        next(a)
        started[q] = [b, a]

    def advance(q, rounds):
        for _ in range(rounds):
            started[q] = [g for g in started[q] if next(g, True) is None]
        return started[q]

    begin(0, lambda: pl.semaphore_wait(barrier, fsdp + rep - 2))
    for q in range(chunks):
        advance(q, 1)
        if q + 1 < chunks:
            begin(q + 1)
        while advance(q, 1):
            pass
        arrivals[q] = to_owners(q)
        if q == 0:
            load_first.wait()
            load_second.wait()
        if q > 0:
            arrivals[q - 1] = moments(q - 1, arrivals[q - 1])
    arrivals[chunks - 1] = moments(chunks - 1, arrivals[chunks - 1])
    outputs = [
        pltpu.make_async_copy(new_first, new_first_hbm.at[0], out_sem.at[0]),
        pltpu.make_async_copy(new_second, new_second_hbm.at[0], out_sem.at[1]),
    ]
    for copy in outputs:
        copy.start()
    for q in range(chunks):
        to_units(q, arrivals[q])
        rotate_left(q)
        if q > 0:
            finish(q - 1)
    finish(chunks - 1)
    outputs.append(pltpu.make_async_copy(update, update_hbm, out_sem.at[2]))
    outputs[-1].start()

    for copy in sent:
        copy.wait_send()
    for q in range(chunks):

        @pl.when(is_unit(q))
        def _(q=q):
            unit_copy(q, units - 1).wait_send()
            row_copy(q, rep - 1).wait_send()

        @pl.when(jnp.logical_not(is_unit(q)))
        def _(q=q):
            unit_copy(q, units).wait_send()

    for copy in outputs:
        copy.wait()


def body(grad_partial, basis_left, basis_right, owner_table, moment_first, moment_second):
    fsdp = lax.axis_size("fsdp")
    rep = lax.axis_size("rep")
    blocks, size = basis_left.shape[0], basis_left.shape[1]
    slots, rows = moment_first.shape[1], moment_first.shape[2]
    nx = GRID_X
    ny = rep // nx
    width = size // CHUNKS
    half = blocks // 2
    cols = width // LANES
    sizes = (fsdp, nx, ny, CHUNKS, width, blocks, slots)
    anywhere = pl.BlockSpec(memory_space=pl.ANY)

    def vmem(*shape, kind=BF16):
        return pltpu.VMEM(shape, kind)

    tile = (rows, width)
    scratch = [
        vmem(blocks, size, size),
        vmem(blocks, size, size),
        vmem(blocks, size, size),
        vmem(slots, rows, size),
        vmem(slots, rows, size, kind=F32),
        vmem(slots, rows, size),
        vmem(slots, rows, size, kind=F32),
        vmem(blocks, rows, size),
        vmem(blocks, rows, size, kind=F32),
        vmem(CHUNKS, blocks, nx, ny, *tile),
        vmem(CHUNKS, 2, nx // 2, half, ny, *tile),
        vmem(CHUNKS, 2, ny // 2, half, *tile),
        vmem(CHUNKS, 2, ny // 2, blocks - half, nx, *tile),
        vmem(CHUNKS, 2, nx // 2, blocks - half, *tile),
        vmem(CHUNKS, blocks, *tile),
        [vmem(fsdp, *tile) for _ in range(CHUNKS)],
        [vmem(fsdp, *tile) for _ in range(CHUNKS)],
        [vmem(fsdp, *tile) for _ in range(CHUNKS)],
        [vmem(fsdp, *tile) for _ in range(CHUNKS)],
        (
            vmem(CHUNKS * blocks * cols, rows, LANES),
            [vmem(slots, *tile) for _ in range(CHUNKS)],
        ),
        vmem(rep, rows, LANES),
        vmem(rep, rows, LANES),
        vmem(CHUNKS * blocks * cols, rows, LANES),
        pltpu.SMEM((2 * fsdp + slots + 1,), jnp.int32),
        pltpu.SemaphoreType.DMA((4, blocks)),
        pltpu.SemaphoreType.DMA((3,)),
        pltpu.SemaphoreType.DMA((CHUNKS, 4, 2, ny // 2)),
        pltpu.SemaphoreType.DMA((CHUNKS, 4, 2, ny // 2)),
        pltpu.SemaphoreType.DMA((CHUNKS, 4)),
        pltpu.SemaphoreType.DMA((CHUNKS, 4)),
    ]
    return pl.pallas_call(
        functools.partial(kernel, sizes),
        out_shape=(
            jax.ShapeDtypeStruct((blocks, rows, size), BF16),
            jax.ShapeDtypeStruct(moment_first.shape, BF16),
            jax.ShapeDtypeStruct(moment_second.shape, F32),
        ),
        in_specs=[
            anywhere,
            anywhere,
            anywhere,
            pl.BlockSpec(memory_space=pltpu.SMEM),
            anywhere,
            anywhere,
        ],
        out_specs=(anywhere,) * 3,
        scratch_shapes=scratch,
        compiler_params=pltpu.CompilerParams(
            collective_id=0, has_side_effects=True, vmem_limit_bytes=56 * 1024 * 1024
        ),
    )(grad_partial, basis_left, basis_right, owner_table, moment_first, moment_second)


def solution(mesh):
    placed = (
        P("rep", "fsdp", None, None),
        P("fsdp", None, None),
        P("fsdp", None, None),
        P(),
        P("fsdp", None, "rep", None),
        P("fsdp", None, "rep", None),
    )
    return jax.shard_map(
        body,
        mesh=mesh,
        in_specs=placed,
        out_specs=(
            P("fsdp", "rep", None),
            P("fsdp", None, "rep", None),
            P("fsdp", None, "rep", None),
        ),
        check_vma=False,
    )
```

```python
import functools

import jax
import jax.numpy as jnp
from jax import lax
from jax.experimental import pallas as pl
from jax.experimental.pallas import tpu as pltpu
from jax.sharding import PartitionSpec as P

BETA_ONE = 0.9
BETA_TWO = 0.95
EPSILON = 1e-08
GRID_X = 4
LANES = 128
CHUNKS = 2
F32 = jnp.float32
BF16 = jnp.bfloat16


def kernel(
    sizes,
    grad_hbm,
    left_hbm,
    right_hbm,
    table,
    first_hbm,
    second_hbm,
    update,
    new_first,
    new_second,
    grad,
    left,
    right,
    first,
    second,
    total_back,
    part_a,
    part_b,
    ring_a_x,
    direct_a,
    ring_b_y,
    direct_b,
    reduced,
    outgoing,
    incoming,
    sendback,
    comeback,
    tiles,
    gathered,
    product,
    rows_in,
    slot_table,
    in_sem,
    ring_send,
    ring_recv,
    swap_send,
    swap_recv,
):
    fsdp, nx, ny, chunks, width, blocks, slots = sizes
    rep = nx * ny
    cols = width // LANES
    half_blocks = blocks // 2
    units = blocks * cols
    shard = lax.axis_index("fsdp")
    replica = lax.axis_index("rep")
    my_x = replica // ny
    my_y = replica % ny

    def at_fsdp(step):
        return {"fsdp": (shard + step) % fsdp}

    def at_rep(step):
        return {"rep": (replica + step) % rep}

    def load(k, which):
        source, target = ((grad_hbm.at[0], grad), (left_hbm, left), (right_hbm, right))[which]
        return pltpu.make_async_copy(source.at[k], target.at[k], in_sem.at[which, k])

    def load_blocks(low, high):
        for k in range(low, high):
            for which in (0, 2, 1):
                load(k, which).start()

    load_blocks(half_blocks, blocks)
    barrier = pltpu.get_barrier_semaphore()

    def greet(axis):
        def body(step, carry):
            pl.semaphore_signal(
                barrier, inc=1, device_id=axis(step), device_id_type=pl.DeviceIdType.MESH
            )
            return carry

        return body

    lax.fori_loop(1, fsdp, greet(at_fsdp), 0)
    lax.fori_loop(1, rep, greet(at_rep), 0)
    load_blocks(0, half_blocks)
    load_first = pltpu.make_async_copy(first_hbm.at[0], first, in_sem.at[3, 0])
    load_second = pltpu.make_async_copy(second_hbm.at[0], second, in_sem.at[3, 1])
    load_first.start()
    load_second.start()

    def rotate(low, high):
        def body(k, carry):
            for which in (0, 2, 1):
                load(k, which).wait()
            right_part = jnp.dot(grad[k], right[k], preferred_element_type=F32)
            rotated = lax.dot_general(
                left[k],
                right_part.astype(BF16),
                (((0,), (0,)), ((), ())),
                preferred_element_type=F32,
            ).astype(BF16)
            for q in range(chunks):
                rows = rotated[:, q * width : (q + 1) * width].reshape(nx, ny, 16, width)
                if low == 0:
                    for x in range(nx):
                        part_a[q, x, k] = rows[x]
                else:
                    for y in range(ny):
                        part_b[q, y, k - low] = rows[:, y]
            return carry

        lax.fori_loop(low, high, body, 0)

    def remote(source, target, send, recv, device):
        return pltpu.make_async_remote_copy(
            src_ref=source,
            dst_ref=target,
            send_sem=send,
            recv_sem=recv,
            device_id=device,
            device_id_type=pl.DeviceIdType.MESH,
        )

    sent = []

    def ring(count, position, piece, landing, sems, device):
        reach = count // 2
        flying = {}

        def copy(way, step):
            there = (position + way * (reach - step + 1) + count) % count
            side = 0 if way > 0 else 1
            cut = None if step > 1 else side
            return remote(
                piece(there, cut),
                landing(side, step - 1, cut),
                ring_send.at[sems + (side, step - 1)],
                ring_recv.at[sems + (side, step - 1)],
                device(way),
            )

        for step in range(1, reach + 1):
            for way in (1, -1):
                side = 0 if way > 0 else 1
                if step > 1:
                    flying[way].wait_recv()
                    there = (position + way * (reach - step + 1) + count) % count
                    cut = side if step == 2 else None
                    held = piece(there, cut)
                    held[...] = held[...] + landing(side, step - 2, cut)[...]
                flying[way] = copy(way, step)
                flying[way].start()
                sent.append(flying[way])
            yield
        flying[1].wait_recv()
        flying[-1].wait_recv()

    def split(low, count, cut):
        if cut is None:
            return pl.ds(low, count)
        middle = (count + 1) // 2
        return pl.ds(low, middle) if cut == 0 else pl.ds(low + middle, count - middle)

    def along_x(way):
        return {"rep": ((my_x + way + nx) % nx) * ny + my_y}

    def along_y(way):
        return {"rep": my_x * ny + (my_y + way + ny) % ny}

    def total(own, landed):
        result = own.astype(F32)
        for value in landed:
            result = result + value.astype(F32)
        return result

    def direct(count, piece, landing, sems, device):
        for step in sorted(range(1, count), key=lambda step: -min(step, count - step)):
            remote(
                piece(step),
                landing.at[step],
                swap_send.at[sems],
                swap_recv.at[sems],
                device(step),
            ).start()
        others = landing.at[pl.ds(1, count - 1)]
        whole = remote(others, others, swap_send.at[sems], swap_recv.at[sems], device(1))
        sent.append(whole)
        return whole

    def sum_a(q):
        yield from ring(
            nx,
            my_x,
            lambda there, cut: part_a.at[q, there, :, split(0, ny, cut)],
            lambda side, step, cut: ring_a_x.at[q, side, step, :, split(0, ny, cut)],
            (q, 0),
            along_x,
        )
        for k in range(half_blocks):
            part_a[q, my_x, k] = total(
                part_a[q, my_x, k], [ring_a_x[q, side, nx // 2 - 1, k] for side in (0, 1)]
            ).astype(BF16)
        whole = direct(
            ny,
            lambda step: part_a.at[q, my_x, :, (my_y + step) % ny],
            direct_a.at[q],
            (q, 4),
            along_y,
        )
        yield
        whole.wait_recv()
        for k in range(half_blocks):
            reduced[q, k] = total(
                part_a[q, my_x, k, my_y], [direct_a[q, step, k] for step in range(1, ny)]
            ).astype(BF16)

    def sum_b(q):
        yield from ring(
            ny,
            my_y,
            lambda there, cut: part_b.at[q, there, :, split(0, nx, cut)],
            lambda side, step, cut: ring_b_y.at[q, side, step, :, split(0, nx, cut)],
            (q, 1),
            along_y,
        )
        for k in range(blocks - half_blocks):
            part_b[q, my_y, k] = total(
                part_b[q, my_y, k],
                [ring_b_y[q, side, ny // 2 - 1, k] for side in (0, 1)],
            ).astype(BF16)
        whole = direct(
            nx,
            lambda step: part_b.at[q, my_y, :, (my_x + step) % nx],
            direct_b.at[q],
            (q, 5),
            along_x,
        )
        yield
        whole.wait_recv()
        for k in range(blocks - half_blocks):
            reduced[q, half_blocks + k] = total(
                part_b[q, my_y, k, my_x],
                [direct_b[q, step, k] for step in range(1, nx)],
            ).astype(BF16)

    def lookups():
        def of_shard(other, carry):
            rank, picks = carry
            named = jnp.int32(0)
            for k in range(blocks):
                named += (table[other * blocks + k] == shard).astype(jnp.int32)
            slot_table[other] = jnp.minimum(rank, slots - 1)
            away = (shard - other + fsdp) % fsdp
            picks = tuple(
                jnp.where((named > 0) & (rank == j), away, picks[j]) for j in range(slots)
            )
            return rank + named, picks

        count, picks = lax.fori_loop(
            0, fsdp, of_shard, (jnp.int32(0), (jnp.int32(0),) * slots)
        )
        for j in range(slots):
            slot_table[2 * fsdp + j] = picks[j]
        slot_table[2 * fsdp + slots] = count

        def of_owner(owner, carry):
            block = jnp.int32(0)
            for k in range(blocks):
                block = jnp.where(table[shard * blocks + k] == owner, k, block)
            slot_table[fsdp + owner] = block
            return carry

        lax.fori_loop(0, fsdp, of_owner, 0)

    def swap(q, which, source, target, pick):
        def start(turn, carry):
            pair = turn // 2
            across = fsdp // 4 + jnp.where(pair % 2 == 0, pair // 2, -(pair + 1) // 2)
            step = 2 * across + 1 - turn % 2
            source[step] = pick((shard + step) % fsdp)
            remote(
                source.at[step],
                target.at[step],
                swap_send.at[q, which],
                swap_recv.at[q, which],
                at_fsdp(step),
            ).start()
            return carry

        lax.fori_loop(0, fsdp - 1, start, 0)
        target[0] = pick(shard)
        others = pl.ds(1, fsdp - 1)
        whole = remote(
            source.at[others],
            target.at[others],
            swap_send.at[q, which],
            swap_recv.at[q, which],
            at_fsdp(1),
        )
        sent.append(whole)
        return whole

    def to_owners(q):
        return swap(
            q, 0, outgoing[q], incoming[q], lambda owner: reduced[q, slot_table[fsdp + owner]]
        )

    def moment_of(q, j):
        columns = pl.ds(q * width, width)
        gradient = incoming[q][slot_table[2 * fsdp + j]].astype(F32)
        first_old = first[j, :, columns].astype(F32)
        second_old = second[j, :, columns]
        first_now = BETA_ONE * first_old + (1.0 - BETA_ONE) * gradient
        second_now = BETA_TWO * second_old + (1.0 - BETA_TWO) * gradient * gradient
        return first_old, second_old, first_now, second_now

    def to_shards(q):
        direction = tiles[1][q]

        def body(j, carry):
            _, _, first_now, second_now = moment_of(q, j)
            direction[j] = (first_now / (jnp.sqrt(second_now) + EPSILON)).astype(BF16)
            return carry

        lax.fori_loop(0, slots, body, 0)
        return swap(q, 1, sendback[q], comeback[q], lambda other: direction[slot_table[other]])

    def keep_moments(q):
        columns = pl.ds(q * width, width)
        count = slot_table[2 * fsdp + slots]

        def body(j, carry):
            first_old, second_old, first_now, second_now = moment_of(q, j)
            used = j < count
            new_first[0, j, :, columns] = jnp.where(used, first_now, first_old).astype(BF16)
            new_second[0, j, :, columns] = jnp.where(used, second_now, second_old)
            return carry

        lax.fori_loop(0, slots, body, 0)

    def to_units(q):
        piece = tiles[0]
        base = q * units

        for k in range(blocks):
            away = (shard - table[shard * blocks + k] + fsdp) % fsdp
            rows = comeback[q][away]
            for c in range(cols):
                piece[base + k * cols + c] = rows[:, c * LANES : (c + 1) * LANES]

        def start(unit, carry):
            @pl.when(unit != replica)
            def _():
                remote(
                    piece.at[unit],
                    gathered.at[replica],
                    swap_send.at[q, 2],
                    swap_recv.at[q, 2],
                    {"rep": unit},
                ).start()

            @pl.when(unit == replica)
            def _():
                gathered[unit] = piece[unit]

            return carry

        lax.fori_loop(base, base + units, start, 0)

    def unit_copy(q, count):
        return remote(
            gathered.at[pl.ds(0, count)],
            gathered.at[pl.ds(0, count)],
            swap_send.at[q, 2],
            swap_recv.at[q, 2],
            at_rep(1),
        )

    def row_copy(q, count):
        return remote(
            product.at[pl.ds(0, count)],
            product.at[pl.ds(0, count)],
            swap_send.at[q, 3],
            swap_recv.at[q, 3],
            at_rep(1),
        )

    def is_unit(q):
        return (replica >= q * units) & (replica < (q + 1) * units)

    def rotate_left(q):
        @pl.when(is_unit(q))
        def _():
            unit_copy(q, rep - 1).wait_recv()
            block = (replica - q * units) // cols
            back = jnp.dot(
                left[block],
                gathered[...].reshape(rep * 16, LANES),
                preferred_element_type=F32,
            )
            product[...] = back.astype(BF16).reshape(rep, 16, LANES)

            def start(step, carry):
                other = (replica + step) % rep
                remote(
                    product.at[other],
                    rows_in.at[replica],
                    swap_send.at[q, 3],
                    swap_recv.at[q, 3],
                    {"rep": other},
                ).start()
                return carry

            lax.fori_loop(1, rep, start, 0)
            rows_in[replica] = product[replica]

    def finish(q):
        @pl.when(is_unit(q))
        def _():
            row_copy(q, units - 1).wait_recv()

        @pl.when(jnp.logical_not(is_unit(q)))
        def _():
            row_copy(q, units).wait_recv()

        base = q * units
        for k in range(blocks):
            rows = jnp.concatenate([rows_in[base + k * cols + c] for c in range(cols)], axis=1)
            back = lax.dot_general(
                rows,
                right[k, :, q * width : (q + 1) * width],
                (((1,), (1,)), ((), ())),
                preferred_element_type=F32,
            )
            if q > 0:
                back = back + total_back[k]
            if q < chunks - 1:
                total_back[k] = back
            else:
                update[k] = back.astype(BF16)

    scope = jax.named_scope
    each = range(chunks)
    with scope("rotate_b"):
        rotate(half_blocks, blocks)
    with scope("greeting"):
        pl.semaphore_wait(barrier, fsdp + rep - 2)
    b = [sum_b(q) for q in each]
    for q in each:
        next(b[q])
    with scope("rotate_a"):
        rotate(0, half_blocks)
    a = [sum_a(q) for q in each]
    for q in each:
        next(a[q])
    turns = {}

    def go(*names):
        for name in names:
            turns[name] = turns.get(name, 1) + 1
            with scope(f"{name}_turn{turns[name]}"):
                next((a if name[0] == "a" else b)[int(name[1])], None)

    go("b0", "b1")
    with scope("lookups"):
        lookups()
    go("a0", "b0", "a1", "b1", "b0", "a0", "b1", "a1", "b0")
    arrivals = []
    for q in each:
        if q > 0:
            go(f"b{q}")
        go(f"a{q}", f"b{q}")
        with scope(f"to_owners{q}"):
            arrivals.append(to_owners(q))
    load_first.wait()
    load_second.wait()
    returns = []
    for q in each:
        with scope(f"wait_owners{q}"):
            arrivals[q].wait_recv()
        with scope(f"to_shards{q}"):
            returns.append(to_shards(q))
    with scope("keep_moments"):
        for q in each:
            keep_moments(q)
    for q in each:
        with scope(f"wait_shards{q}"):
            returns[q].wait_recv()
        with scope(f"to_units{q}"):
            to_units(q)
    for q in each:
        with scope(f"rotate_left{q}"):
            rotate_left(q)
    for q in range(chunks - 1):
        with scope(f"finish{q}"):
            finish(q)

    with scope("sent"):
        for copy in sent:
            copy.wait_send()
    with scope(f"finish{chunks - 1}"):
        finish(chunks - 1)
    for q in each:

        @pl.when(is_unit(q))
        def _(q=q):
            unit_copy(q, units - 1).wait_send()
            row_copy(q, rep - 1).wait_send()

        @pl.when(jnp.logical_not(is_unit(q)))
        def _(q=q):
            unit_copy(q, units).wait_send()


def copy_kernel(*refs):
    count = len(refs) // 2
    sources, targets, sems = refs[:count], refs[count : 2 * count], refs[-1]
    copies = [
        pltpu.make_async_copy(source, target, sems.at[i])
        for i, (source, target) in enumerate(zip(sources, targets))
    ]
    for copy in copies:
        copy.start()
    for copy in copies:
        copy.wait()


def body(grad_partial, basis_left, basis_right, owner_table, moment_first, moment_second):
    fsdp = lax.axis_size("fsdp")
    rep = lax.axis_size("rep")
    blocks, size = basis_left.shape[0], basis_left.shape[1]
    slots, rows = moment_first.shape[1], moment_first.shape[2]
    nx = GRID_X
    ny = rep // nx
    width = size // CHUNKS
    half = blocks // 2
    cols = width // LANES
    sizes = (fsdp, nx, ny, CHUNKS, width, blocks, slots)
    anywhere = pl.BlockSpec(memory_space=pl.ANY)

    def vmem(*shape, kind=BF16):
        return pltpu.VMEM(shape, kind)

    tile = (rows, width)
    scratch = [
        vmem(blocks, size, size),
        vmem(blocks, size, size),
        vmem(blocks, size, size),
        vmem(slots, rows, size),
        vmem(slots, rows, size, kind=F32),
        vmem(blocks, rows, size, kind=F32),
        vmem(CHUNKS, nx, half, ny, *tile),
        vmem(CHUNKS, ny, blocks - half, nx, *tile),
        vmem(CHUNKS, 2, nx // 2, half, ny, *tile),
        vmem(CHUNKS, ny, half, *tile),
        vmem(CHUNKS, 2, ny // 2, blocks - half, nx, *tile),
        vmem(CHUNKS, nx, blocks - half, *tile),
        vmem(CHUNKS, blocks, *tile),
        [vmem(fsdp, *tile) for _ in range(CHUNKS)],
        [vmem(fsdp, *tile) for _ in range(CHUNKS)],
        [vmem(fsdp, *tile) for _ in range(CHUNKS)],
        [vmem(fsdp, *tile) for _ in range(CHUNKS)],
        (
            vmem(CHUNKS * blocks * cols, rows, LANES),
            [vmem(slots, *tile) for _ in range(CHUNKS)],
        ),
        vmem(rep, rows, LANES),
        vmem(rep, rows, LANES),
        vmem(CHUNKS * blocks * cols, rows, LANES),
        pltpu.SMEM((2 * fsdp + slots + 1,), jnp.int32),
        pltpu.SemaphoreType.DMA((4, blocks)),
        pltpu.SemaphoreType.DMA((CHUNKS, 2, 2, ny // 2)),
        pltpu.SemaphoreType.DMA((CHUNKS, 2, 2, ny // 2)),
        pltpu.SemaphoreType.DMA((CHUNKS, 6)),
        pltpu.SemaphoreType.DMA((CHUNKS, 6)),
    ]
    results = pl.pallas_call(
        functools.partial(kernel, sizes),
        out_shape=(
            pltpu.VMEM((blocks, rows, size), BF16),
            pltpu.VMEM(moment_first.shape, BF16),
            pltpu.VMEM(moment_second.shape, F32),
        ),
        in_specs=[
            anywhere,
            anywhere,
            anywhere,
            pl.BlockSpec(memory_space=pltpu.SMEM),
            anywhere,
            anywhere,
        ],
        out_specs=(pl.BlockSpec(memory_space=pltpu.VMEM),) * 3,
        scratch_shapes=scratch,
        compiler_params=pltpu.CompilerParams(
            collective_id=0, has_side_effects=True, vmem_limit_bytes=56 * 1024 * 1024
        ),
    )(grad_partial, basis_left, basis_right, owner_table, moment_first, moment_second)
    return pl.pallas_call(
        copy_kernel,
        out_shape=tuple(jax.ShapeDtypeStruct(r.shape, r.dtype) for r in results),
        in_specs=[pl.BlockSpec(memory_space=pltpu.VMEM)] * 3,
        out_specs=(pl.BlockSpec(memory_space=pltpu.HBM),) * 3,
        scratch_shapes=[pltpu.SemaphoreType.DMA((3,))],
    )(*[pltpu.with_memory_space_constraint(r, pltpu.VMEM) for r in results])


def solution(mesh):
    placed = (
        P("rep", "fsdp", None, None),
        P("fsdp", None, None),
        P("fsdp", None, None),
        P(),
        P("fsdp", None, "rep", None),
        P("fsdp", None, "rep", None),
    )
    return jax.shard_map(
        body,
        mesh=mesh,
        in_specs=placed,
        out_specs=(
            P("fsdp", "rep", None),
            P("fsdp", None, "rep", None),
            P("fsdp", None, "rep", None),
        ),
        check_vma=False,
    )
```

```python
import functools

import jax
import jax.numpy as jnp
from jax import lax
from jax.experimental import pallas as pl
from jax.experimental.pallas import tpu as pltpu
from jax.sharding import PartitionSpec as P

BETA_ONE = 0.9
BETA_TWO = 0.95
EPSILON = 1e-08
GRID_X = 4
LANES = 128
CHUNKS = 2
F32 = jnp.float32
BF16 = jnp.bfloat16


def kernel(
    sizes,
    grad_hbm,
    left_hbm,
    right_hbm,
    table,
    first_hbm,
    second_hbm,
    update,
    new_first,
    new_second,
    grad,
    left,
    right,
    first,
    second,
    total_back,
    part_a,
    part_b,
    ring_a_x,
    direct_a,
    ring_b_y,
    direct_b,
    reduced,
    outgoing,
    incoming,
    sendback,
    comeback,
    piece,
    gathered,
    product,
    rows_in,
    slot_table,
    in_sem,
    ring_send,
    ring_recv,
    swap_send,
    swap_recv,
):
    fsdp, nx, ny, chunks, width, blocks, slots = sizes
    rep = nx * ny
    cols = width // LANES
    half_blocks = blocks // 2
    units = blocks * cols
    shard = lax.axis_index("fsdp")
    replica = lax.axis_index("rep")
    my_x = replica // ny
    my_y = replica % ny

    def at_fsdp(step):
        return {"fsdp": (shard + step) % fsdp}

    def at_rep(step):
        return {"rep": (replica + step) % rep}

    def load(k, which):
        source, target = ((grad_hbm.at[0], grad), (left_hbm, left), (right_hbm, right))[which]
        return pltpu.make_async_copy(source.at[k], target.at[k], in_sem.at[which, k])

    def load_blocks(low, high):
        for k in range(low, high):
            for which in (0, 2, 1):
                load(k, which).start()

    load_blocks(half_blocks, blocks)
    barrier = pltpu.get_barrier_semaphore()

    def greet(axis):
        def body(step, carry):
            pl.semaphore_signal(
                barrier, inc=1, device_id=axis(step), device_id_type=pl.DeviceIdType.MESH
            )
            return carry

        return body

    lax.fori_loop(1, fsdp, greet(at_fsdp), 0)
    lax.fori_loop(1, rep, greet(at_rep), 0)
    load_first = pltpu.make_async_copy(first_hbm.at[0], first, in_sem.at[3, 0])
    load_second = pltpu.make_async_copy(second_hbm.at[0], second, in_sem.at[3, 1])
    load_first.start()
    load_second.start()
    load_blocks(0, half_blocks)

    def rotate(low, high):
        def body(k, carry):
            for which in (0, 2, 1):
                load(k, which).wait()
            right_part = jnp.dot(grad[k], right[k], preferred_element_type=F32)
            rotated = lax.dot_general(
                left[k],
                right_part.astype(BF16),
                (((0,), (0,)), ((), ())),
                preferred_element_type=F32,
            ).astype(BF16)
            for q in range(chunks):
                rows = rotated[:, q * width : (q + 1) * width].reshape(nx, ny, 16, width)
                if low == 0:
                    for x in range(nx):
                        part_a[q, x, k] = rows[x]
                else:
                    for y in range(ny):
                        part_b[q, y, k - low] = rows[:, y]
            return carry

        lax.fori_loop(low, high, body, 0)

    def remote(source, target, send, recv, device):
        return pltpu.make_async_remote_copy(
            src_ref=source,
            dst_ref=target,
            send_sem=send,
            recv_sem=recv,
            device_id=device,
            device_id_type=pl.DeviceIdType.MESH,
        )

    sent = []

    def ring(count, position, piece, landing, sems, device):
        reach = count // 2
        flying = {}

        def copy(way, step):
            there = (position + way * (reach - step + 1) + count) % count
            side = 0 if way > 0 else 1
            cut = None if step > 1 else side
            return remote(
                piece(there, cut),
                landing(side, step - 1, cut),
                ring_send.at[sems + (side, step - 1)],
                ring_recv.at[sems + (side, step - 1)],
                device(way),
            )

        for step in range(1, reach + 1):
            for way in (1, -1):
                side = 0 if way > 0 else 1
                if step > 1:
                    flying[way].wait_recv()
                    there = (position + way * (reach - step + 1) + count) % count
                    cut = side if step == 2 else None
                    held = piece(there, cut)
                    held[...] = held[...] + landing(side, step - 2, cut)[...]
                flying[way] = copy(way, step)
                flying[way].start()
                sent.append(flying[way])
            yield
        flying[1].wait_recv()
        flying[-1].wait_recv()

    def split(low, count, cut):
        if cut is None:
            return pl.ds(low, count)
        middle = (count + 1) // 2
        return pl.ds(low, middle) if cut == 0 else pl.ds(low + middle, count - middle)

    def along_x(way):
        return {"rep": ((my_x + way + nx) % nx) * ny + my_y}

    def along_y(way):
        return {"rep": my_x * ny + (my_y + way + ny) % ny}

    def total(own, landed):
        result = own.astype(F32)
        for value in landed:
            result = result + value.astype(F32)
        return result

    def direct(count, piece, landing, sems, device):
        for step in sorted(range(1, count), key=lambda step: -min(step, count - step)):
            remote(
                piece(step),
                landing.at[step],
                swap_send.at[sems],
                swap_recv.at[sems],
                device(step),
            ).start()
        others = landing.at[pl.ds(1, count - 1)]
        whole = remote(others, others, swap_send.at[sems], swap_recv.at[sems], device(1))
        sent.append(whole)
        return whole

    def sum_a(q):
        yield from ring(
            nx,
            my_x,
            lambda there, cut: part_a.at[q, there, :, split(0, ny, cut)],
            lambda side, step, cut: ring_a_x.at[q, side, step, :, split(0, ny, cut)],
            (q, 0),
            along_x,
        )
        for k in range(half_blocks):
            part_a[q, my_x, k] = total(
                part_a[q, my_x, k], [ring_a_x[q, side, nx // 2 - 1, k] for side in (0, 1)]
            ).astype(BF16)
        whole = direct(
            ny,
            lambda step: part_a.at[q, my_x, :, (my_y + step) % ny],
            direct_a.at[q],
            (q, 4),
            along_y,
        )
        yield
        whole.wait_recv()
        for k in range(half_blocks):
            reduced[q, k] = total(
                part_a[q, my_x, k, my_y], [direct_a[q, step, k] for step in range(1, ny)]
            ).astype(BF16)

    def sum_b(q):
        yield from ring(
            ny,
            my_y,
            lambda there, cut: part_b.at[q, there, :, split(0, nx, cut)],
            lambda side, step, cut: ring_b_y.at[q, side, step, :, split(0, nx, cut)],
            (q, 1),
            along_y,
        )
        for k in range(blocks - half_blocks):
            part_b[q, my_y, k] = total(
                part_b[q, my_y, k],
                [ring_b_y[q, side, ny // 2 - 1, k] for side in (0, 1)],
            ).astype(BF16)
        whole = direct(
            nx,
            lambda step: part_b.at[q, my_y, :, (my_x + step) % nx],
            direct_b.at[q],
            (q, 5),
            along_x,
        )
        yield
        whole.wait_recv()
        for k in range(blocks - half_blocks):
            reduced[q, half_blocks + k] = total(
                part_b[q, my_y, k, my_x],
                [direct_b[q, step, k] for step in range(1, nx)],
            ).astype(BF16)

    def ranks():
        def of_shard(other, rank):
            slot_table[other] = rank
            for k in range(blocks):
                rank += (table[other * blocks + k] == shard).astype(jnp.int32)
            return rank

        slot_table[2 * fsdp + slots] = lax.fori_loop(0, fsdp, of_shard, jnp.int32(0))

    def lookups():
        def of_shard(other, picks):
            rank = slot_table[other]
            away = (shard - other + fsdp) % fsdp
            return tuple(jnp.where(rank == j, away, picks[j]) for j in range(slots))

        picks = lax.fori_loop(0, fsdp, of_shard, (jnp.int32(0),) * slots)
        for j in range(slots):
            slot_table[2 * fsdp + j] = picks[j]

        def of_owner(owner, carry):
            block = jnp.int32(0)
            for k in range(blocks):
                block = jnp.where(table[shard * blocks + k] == owner, k, block)
            slot_table[fsdp + owner] = block
            return carry

        lax.fori_loop(0, fsdp, of_owner, 0)

    def swap(q, which, source, target, fill):
        def start(turn, carry):
            pair = turn // 2
            across = fsdp // 4 + jnp.where(pair % 2 == 0, pair // 2, -(pair + 1) // 2)
            step = 2 * across + 1 - turn % 2
            fill(source.at[step], (shard + step) % fsdp)
            remote(
                source.at[step],
                target.at[step],
                swap_send.at[q, which],
                swap_recv.at[q, which],
                at_fsdp(step),
            ).start()
            return carry

        lax.fori_loop(0, fsdp - 1, start, 0)
        fill(target.at[0], shard)
        others = pl.ds(1, fsdp - 1)
        whole = remote(
            source.at[others],
            target.at[others],
            swap_send.at[q, which],
            swap_recv.at[q, which],
            at_fsdp(1),
        )
        sent.append(whole)
        return whole

    def to_owners(q):
        def fill(slot, owner):
            slot[...] = reduced[q, slot_table[fsdp + owner]]

        return swap(q, 0, outgoing[q], incoming[q], fill)

    def to_shards(q):
        columns = pl.ds(q * width, width)

        def fill(slot, other):
            held = jnp.minimum(slot_table[other], slots - 1)
            slot[0] = first[held, :, columns]
            slot[1] = second[held, :, columns].astype(BF16)

        return swap(q, 1, sendback[q], comeback[q], fill)

    def advanced(first_old, second_old, gradient):
        first_now = BETA_ONE * first_old + (1.0 - BETA_ONE) * gradient
        second_now = BETA_TWO * second_old + (1.0 - BETA_TWO) * gradient * gradient
        return first_now, second_now

    def keep_moments(q):
        columns = pl.ds(q * width, width)
        count = slot_table[2 * fsdp + slots]

        def body(j, carry):
            gradient = incoming[q][slot_table[2 * fsdp + j]].astype(F32)
            first_old = first[j, :, columns].astype(F32)
            second_old = second[j, :, columns]
            first_now, second_now = advanced(first_old, second_old, gradient)
            used = j < count
            new_first[0, j, :, columns] = jnp.where(used, first_now, first_old).astype(BF16)
            new_second[0, j, :, columns] = jnp.where(used, second_now, second_old)
            return carry

        lax.fori_loop(0, slots, body, 0)

    def to_units(q):
        base = q * units

        for k in range(blocks):
            away = (shard - table[shard * blocks + k] + fsdp) % fsdp
            first_now, second_now = advanced(
                comeback[q][away, 0].astype(F32),
                comeback[q][away, 1].astype(F32),
                reduced[q, k].astype(F32),
            )
            rows = (first_now / (jnp.sqrt(second_now) + EPSILON)).astype(BF16)
            for c in range(cols):
                piece[base + k * cols + c] = rows[:, c * LANES : (c + 1) * LANES]

        def start(unit, carry):
            @pl.when(unit != replica)
            def _():
                remote(
                    piece.at[unit],
                    gathered.at[replica],
                    swap_send.at[q, 2],
                    swap_recv.at[q, 2],
                    {"rep": unit},
                ).start()

            @pl.when(unit == replica)
            def _():
                gathered[unit] = piece[unit]

            return carry

        lax.fori_loop(base, base + units, start, 0)

    def unit_copy(q, count):
        return remote(
            gathered.at[pl.ds(0, count)],
            gathered.at[pl.ds(0, count)],
            swap_send.at[q, 2],
            swap_recv.at[q, 2],
            at_rep(1),
        )

    def row_copy(q, count):
        return remote(
            product.at[pl.ds(0, count)],
            product.at[pl.ds(0, count)],
            swap_send.at[q, 3],
            swap_recv.at[q, 3],
            at_rep(1),
        )

    def is_unit(q):
        return (replica >= q * units) & (replica < (q + 1) * units)

    def rotate_left(q):
        @pl.when(is_unit(q))
        def _():
            unit_copy(q, rep - 1).wait_recv()
            block = (replica - q * units) // cols
            back = jnp.dot(
                left[block],
                gathered[...].reshape(rep * 16, LANES),
                preferred_element_type=F32,
            )
            product[...] = back.astype(BF16).reshape(rep, 16, LANES)

            def start(step, carry):
                other = (replica + step) % rep
                remote(
                    product.at[other],
                    rows_in.at[replica],
                    swap_send.at[q, 3],
                    swap_recv.at[q, 3],
                    {"rep": other},
                ).start()
                return carry

            lax.fori_loop(1, rep, start, 0)
            rows_in[replica] = product[replica]

    def finish(q):
        @pl.when(is_unit(q))
        def _():
            row_copy(q, units - 1).wait_recv()

        @pl.when(jnp.logical_not(is_unit(q)))
        def _():
            row_copy(q, units).wait_recv()

        base = q * units
        for k in range(blocks):
            rows = jnp.concatenate([rows_in[base + k * cols + c] for c in range(cols)], axis=1)
            back = lax.dot_general(
                rows,
                right[k, :, q * width : (q + 1) * width],
                (((1,), (1,)), ((), ())),
                preferred_element_type=F32,
            )
            if q > 0:
                back = back + total_back[k]
            if q < chunks - 1:
                total_back[k] = back
            else:
                update[k] = back.astype(BF16)

    scope = jax.named_scope
    each = range(chunks)
    with scope("rotate_b"):
        rotate(half_blocks, blocks)
    with scope("greeting"):
        pl.semaphore_wait(barrier, fsdp + rep - 2)
    b = [sum_b(q) for q in each]
    for q in each:
        next(b[q])
    with scope("ranks"):
        ranks()
        load_first.wait()
        load_second.wait()
    with scope("to_shards0"):
        moments = [to_shards(0)]
    with scope("rotate_a"):
        rotate(0, half_blocks)
    a = [sum_a(q) for q in each]
    for q in each:
        next(a[q])
    turns = {}

    def go(*names):
        for name in names:
            turns[name] = turns.get(name, 1) + 1
            with scope(f"{name}_turn{turns[name]}"):
                next((a if name[0] == "a" else b)[int(name[1])], None)

    go("b0", "b1")
    for q in range(1, chunks):
        with scope(f"to_shards{q}"):
            moments.append(to_shards(q))
    go("a0", "b0", "a1", "b1")
    with scope("lookups"):
        lookups()
    go("b0", "b1", "a0", "a1", "b0", "b1")
    arrivals = []
    for q in each:
        go(f"a{q}", f"b{q}")
        with scope(f"wait_moments{q}"):
            moments[q].wait_recv()
        with scope(f"to_units{q}"):
            to_units(q)
        with scope(f"to_owners{q}"):
            arrivals.append(to_owners(q))
    for q in each:
        with scope(f"rotate_left{q}"):
            rotate_left(q)
    for q in each:
        with scope(f"wait_owners{q}"):
            arrivals[q].wait_recv()
        with scope(f"keep_moments{q}"):
            keep_moments(q)
        if q < chunks - 1:
            with scope(f"finish{q}"):
                finish(q)

    with scope("sent"):
        for copy in sent:
            copy.wait_send()
    with scope(f"finish{chunks - 1}"):
        finish(chunks - 1)
    for q in each:

        @pl.when(is_unit(q))
        def _(q=q):
            unit_copy(q, units - 1).wait_send()
            row_copy(q, rep - 1).wait_send()

        @pl.when(jnp.logical_not(is_unit(q)))
        def _(q=q):
            unit_copy(q, units).wait_send()


def copy_kernel(*refs):
    count = len(refs) // 2
    sources, targets, sems = refs[:count], refs[count : 2 * count], refs[-1]
    copies = [
        pltpu.make_async_copy(source, target, sems.at[i])
        for i, (source, target) in enumerate(zip(sources, targets))
    ]
    for copy in copies:
        copy.start()
    for copy in copies:
        copy.wait()


def body(grad_partial, basis_left, basis_right, owner_table, moment_first, moment_second):
    fsdp = lax.axis_size("fsdp")
    rep = lax.axis_size("rep")
    blocks, size = basis_left.shape[0], basis_left.shape[1]
    slots, rows = moment_first.shape[1], moment_first.shape[2]
    nx = GRID_X
    ny = rep // nx
    width = size // CHUNKS
    half = blocks // 2
    cols = width // LANES
    sizes = (fsdp, nx, ny, CHUNKS, width, blocks, slots)
    anywhere = pl.BlockSpec(memory_space=pl.ANY)

    def vmem(*shape, kind=BF16):
        return pltpu.VMEM(shape, kind)

    tile = (rows, width)
    scratch = [
        vmem(blocks, size, size),
        vmem(blocks, size, size),
        vmem(blocks, size, size),
        vmem(slots, rows, size),
        vmem(slots, rows, size, kind=F32),
        vmem(blocks, rows, size, kind=F32),
        vmem(CHUNKS, nx, half, ny, *tile),
        vmem(CHUNKS, ny, blocks - half, nx, *tile),
        vmem(CHUNKS, 2, nx // 2, half, ny, *tile),
        vmem(CHUNKS, ny, half, *tile),
        vmem(CHUNKS, 2, ny // 2, blocks - half, nx, *tile),
        vmem(CHUNKS, nx, blocks - half, *tile),
        vmem(CHUNKS, blocks, *tile),
        [vmem(fsdp, *tile) for _ in range(CHUNKS)],
        [vmem(fsdp, *tile) for _ in range(CHUNKS)],
        [vmem(fsdp, 2, *tile) for _ in range(CHUNKS)],
        [vmem(fsdp, 2, *tile) for _ in range(CHUNKS)],
        vmem(CHUNKS * blocks * cols, rows, LANES),
        vmem(rep, rows, LANES),
        vmem(rep, rows, LANES),
        vmem(CHUNKS * blocks * cols, rows, LANES),
        pltpu.SMEM((2 * fsdp + slots + 1,), jnp.int32),
        pltpu.SemaphoreType.DMA((4, blocks)),
        pltpu.SemaphoreType.DMA((CHUNKS, 2, 2, ny // 2)),
        pltpu.SemaphoreType.DMA((CHUNKS, 2, 2, ny // 2)),
        pltpu.SemaphoreType.DMA((CHUNKS, 6)),
        pltpu.SemaphoreType.DMA((CHUNKS, 6)),
    ]
    results = pl.pallas_call(
        functools.partial(kernel, sizes),
        out_shape=(
            pltpu.VMEM((blocks, rows, size), BF16),
            pltpu.VMEM(moment_first.shape, BF16),
            pltpu.VMEM(moment_second.shape, F32),
        ),
        in_specs=[
            anywhere,
            anywhere,
            anywhere,
            pl.BlockSpec(memory_space=pltpu.SMEM),
            anywhere,
            anywhere,
        ],
        out_specs=(pl.BlockSpec(memory_space=pltpu.VMEM),) * 3,
        scratch_shapes=scratch,
        compiler_params=pltpu.CompilerParams(
            collective_id=0, has_side_effects=True, vmem_limit_bytes=56 * 1024 * 1024
        ),
    )(grad_partial, basis_left, basis_right, owner_table, moment_first, moment_second)
    return pl.pallas_call(
        copy_kernel,
        out_shape=tuple(jax.ShapeDtypeStruct(r.shape, r.dtype) for r in results),
        in_specs=[pl.BlockSpec(memory_space=pltpu.VMEM)] * 3,
        out_specs=(pl.BlockSpec(memory_space=pltpu.HBM),) * 3,
        scratch_shapes=[pltpu.SemaphoreType.DMA((3,))],
    )(*[pltpu.with_memory_space_constraint(r, pltpu.VMEM) for r in results])


def solution(mesh):
    placed = (
        P("rep", "fsdp", None, None),
        P("fsdp", None, None),
        P("fsdp", None, None),
        P(),
        P("fsdp", None, "rep", None),
        P("fsdp", None, "rep", None),
    )
    return jax.shard_map(
        body,
        mesh=mesh,
        in_specs=placed,
        out_specs=(
            P("fsdp", "rep", None),
            P("fsdp", None, "rep", None),
            P("fsdp", None, "rep", None),
        ),
        check_vma=False,
    )
```

```python
import functools

import jax
import jax.numpy as jnp
from jax import lax
from jax.experimental import pallas as pl
from jax.experimental.pallas import tpu as pltpu
from jax.sharding import PartitionSpec as P

BETA_ONE = 0.9
BETA_TWO = 0.95
EPSILON = 1e-08
GRID_X = 4
LANES = 128
CHUNKS = 2
F32 = jnp.float32
BF16 = jnp.bfloat16


def kernel(
    sizes,
    grad_hbm,
    left_hbm,
    right_hbm,
    table,
    first_hbm,
    second_hbm,
    update,
    new_first,
    new_second,
    grad,
    left,
    right,
    first,
    second,
    total_back,
    part_a,
    part_b,
    ring_a_x,
    direct_a,
    ring_b_y,
    direct_b,
    reduced,
    outgoing,
    incoming,
    sendback,
    comeback,
    piece,
    gathered,
    product,
    rows_in,
    slot_table,
    in_sem,
    ring_send,
    ring_recv,
    swap_send,
    swap_recv,
):
    fsdp, nx, ny, chunks, width, blocks, slots = sizes
    rep = nx * ny
    cols = width // LANES
    half_blocks = blocks // 2
    units = blocks * cols
    shard = lax.axis_index("fsdp")
    replica = lax.axis_index("rep")
    my_x = replica // ny
    my_y = replica % ny

    def at_fsdp(step):
        return {"fsdp": (shard + step) % fsdp}

    def at_rep(step):
        return {"rep": (replica + step) % rep}

    def load(k, which):
        source, target = ((grad_hbm.at[0], grad), (left_hbm, left), (right_hbm, right))[which]
        return pltpu.make_async_copy(source.at[k], target.at[k], in_sem.at[which, k])

    def load_blocks(low, high):
        for k in range(low, high):
            for which in (0, 2, 1):
                load(k, which).start()

    load_blocks(half_blocks, blocks)
    barrier = pltpu.get_barrier_semaphore()

    def greet(axis):
        def body(step, carry):
            pl.semaphore_signal(
                barrier, inc=1, device_id=axis(step), device_id_type=pl.DeviceIdType.MESH
            )
            return carry

        return body

    lax.fori_loop(1, fsdp, greet(at_fsdp), 0)
    lax.fori_loop(1, rep, greet(at_rep), 0)
    load_first = pltpu.make_async_copy(first_hbm.at[0], first, in_sem.at[3, 0])
    load_second = pltpu.make_async_copy(second_hbm.at[0], second, in_sem.at[3, 1])
    load_first.start()
    load_second.start()
    load_blocks(0, half_blocks)

    def rotate(low, high):
        def body(k, carry):
            for which in (0, 2, 1):
                load(k, which).wait()
            right_part = jnp.dot(grad[k], right[k], preferred_element_type=F32)
            rotated = lax.dot_general(
                left[k],
                right_part.astype(BF16),
                (((0,), (0,)), ((), ())),
                preferred_element_type=F32,
            ).astype(BF16)
            for q in range(chunks):
                rows = rotated[:, q * width : (q + 1) * width].reshape(nx, ny, 16, width)
                if low == 0:
                    for x in range(nx):
                        part_a[q, x, k] = rows[x]
                else:
                    for y in range(ny):
                        part_b[q, y, k - low] = rows[:, y]
            return carry

        lax.fori_loop(low, high, body, 0)

    def remote(source, target, send, recv, device):
        return pltpu.make_async_remote_copy(
            src_ref=source,
            dst_ref=target,
            send_sem=send,
            recv_sem=recv,
            device_id=device,
            device_id_type=pl.DeviceIdType.MESH,
        )

    sent = []

    def ring(count, position, piece, landing, sems, device):
        reach = count // 2
        flying = {}

        def copy(way, step):
            there = (position + way * (reach - step + 1) + count) % count
            side = 0 if way > 0 else 1
            cut = None if step > 1 else side
            return remote(
                piece(there, cut),
                landing(side, step - 1, cut),
                ring_send.at[sems + (side, step - 1)],
                ring_recv.at[sems + (side, step - 1)],
                device(way),
            )

        for step in range(1, reach + 1):
            for way in (1, -1):
                side = 0 if way > 0 else 1
                if step > 1:
                    flying[way].wait_recv()
                    there = (position + way * (reach - step + 1) + count) % count
                    cut = side if step == 2 else None
                    held = piece(there, cut)
                    held[...] = held[...] + landing(side, step - 2, cut)[...]
                flying[way] = copy(way, step)
                flying[way].start()
                sent.append(flying[way])
            yield
        flying[1].wait_recv()
        flying[-1].wait_recv()

    def split(low, count, cut):
        if cut is None:
            return pl.ds(low, count)
        middle = (count + 1) // 2
        return pl.ds(low, middle) if cut == 0 else pl.ds(low + middle, count - middle)

    def along_x(way):
        return {"rep": ((my_x + way + nx) % nx) * ny + my_y}

    def along_y(way):
        return {"rep": my_x * ny + (my_y + way + ny) % ny}

    def total(own, landed):
        result = own.astype(F32)
        for value in landed:
            result = result + value.astype(F32)
        return result

    def direct(count, piece, landing, sems, device):
        for step in sorted(range(1, count), key=lambda step: -min(step, count - step)):
            remote(
                piece(step),
                landing.at[step],
                swap_send.at[sems],
                swap_recv.at[sems],
                device(step),
            ).start()
        others = landing.at[pl.ds(1, count - 1)]
        whole = remote(others, others, swap_send.at[sems], swap_recv.at[sems], device(1))
        sent.append(whole)
        return whole

    def sum_a(q):
        yield from ring(
            nx,
            my_x,
            lambda there, cut: part_a.at[q, there, :, split(0, ny, cut)],
            lambda side, step, cut: ring_a_x.at[q, side, step, :, split(0, ny, cut)],
            (q, 0),
            along_x,
        )
        for k in range(half_blocks):
            part_a[q, my_x, k] = total(
                part_a[q, my_x, k], [ring_a_x[q, side, nx // 2 - 1, k] for side in (0, 1)]
            ).astype(BF16)
        whole = direct(
            ny,
            lambda step: part_a.at[q, my_x, :, (my_y + step) % ny],
            direct_a.at[q],
            (q, 4),
            along_y,
        )
        yield
        whole.wait_recv()
        for k in range(half_blocks):
            reduced[q, k] = total(
                part_a[q, my_x, k, my_y], [direct_a[q, step, k] for step in range(1, ny)]
            ).astype(BF16)

    def sum_b(q):
        yield from ring(
            ny,
            my_y,
            lambda there, cut: part_b.at[q, there, :, split(0, nx, cut)],
            lambda side, step, cut: ring_b_y.at[q, side, step, :, split(0, nx, cut)],
            (q, 1),
            along_y,
        )
        for k in range(blocks - half_blocks):
            part_b[q, my_y, k] = total(
                part_b[q, my_y, k],
                [ring_b_y[q, side, ny // 2 - 1, k] for side in (0, 1)],
            ).astype(BF16)
        whole = direct(
            nx,
            lambda step: part_b.at[q, my_y, :, (my_x + step) % nx],
            direct_b.at[q],
            (q, 5),
            along_x,
        )
        yield
        whole.wait_recv()
        for k in range(blocks - half_blocks):
            reduced[q, half_blocks + k] = total(
                part_b[q, my_y, k, my_x],
                [direct_b[q, step, k] for step in range(1, nx)],
            ).astype(BF16)

    def ranks():
        def of_shard(other, rank):
            slot_table[other] = rank
            for k in range(blocks):
                rank += (table[other * blocks + k] == shard).astype(jnp.int32)
            return rank

        slot_table[2 * fsdp + slots] = lax.fori_loop(0, fsdp, of_shard, jnp.int32(0))

    def lookups():
        def of_shard(other, picks):
            rank = slot_table[other]
            away = (shard - other + fsdp) % fsdp
            return tuple(jnp.where(rank == j, away, picks[j]) for j in range(slots))

        picks = lax.fori_loop(0, fsdp, of_shard, (jnp.int32(0),) * slots)
        for j in range(slots):
            slot_table[2 * fsdp + j] = picks[j]

        def of_owner(owner, carry):
            block = jnp.int32(0)
            for k in range(blocks):
                block = jnp.where(table[shard * blocks + k] == owner, k, block)
            slot_table[fsdp + owner] = block
            return carry

        lax.fori_loop(0, fsdp, of_owner, 0)

    def swap(q, which, source, target, fill):
        def start(turn, carry):
            pair = turn // 2
            across = fsdp // 4 + jnp.where(pair % 2 == 0, pair // 2, -(pair + 1) // 2)
            step = 2 * across + 1 - turn % 2
            fill(source.at[step], (shard + step) % fsdp)
            remote(
                source.at[step],
                target.at[step],
                swap_send.at[q, which],
                swap_recv.at[q, which],
                at_fsdp(step),
            ).start()
            return carry

        lax.fori_loop(0, fsdp - 1, start, 0)
        fill(target.at[0], shard)
        others = pl.ds(1, fsdp - 1)
        whole = remote(
            source.at[others],
            target.at[others],
            swap_send.at[q, which],
            swap_recv.at[q, which],
            at_fsdp(1),
        )
        sent.append(whole)
        return whole

    def to_owners(q):
        def fill(slot, owner):
            slot[...] = reduced[q, slot_table[fsdp + owner]]

        return swap(q, 0, outgoing[q], incoming[q], fill)

    def to_shards(q):
        columns = pl.ds(q * width, width)

        def fill(slot, other):
            held = jnp.minimum(slot_table[other], slots - 1)
            slot[0] = first[held, :, columns]
            slot[1] = second[held, :, columns].astype(BF16)

        return swap(q, 1, sendback[q], comeback[q], fill)

    def advanced(first_old, second_old, gradient):
        first_now = BETA_ONE * first_old + (1.0 - BETA_ONE) * gradient
        second_now = BETA_TWO * second_old + (1.0 - BETA_TWO) * gradient * gradient
        return first_now, second_now

    def keep_moments(q):
        columns = pl.ds(q * width, width)
        count = slot_table[2 * fsdp + slots]

        def body(j, carry):
            gradient = incoming[q][slot_table[2 * fsdp + j]].astype(F32)
            first_old = first[j, :, columns].astype(F32)
            second_old = second[j, :, columns]
            first_now, second_now = advanced(first_old, second_old, gradient)
            used = j < count
            new_first[0, j, :, columns] = jnp.where(used, first_now, first_old).astype(BF16)
            new_second[0, j, :, columns] = jnp.where(used, second_now, second_old)
            return carry

        lax.fori_loop(0, slots, body, 0)

    def to_units(q):
        base = q * units

        for k in range(blocks):
            away = (shard - table[shard * blocks + k] + fsdp) % fsdp
            first_now, second_now = advanced(
                comeback[q][away, 0].astype(F32),
                comeback[q][away, 1].astype(F32),
                reduced[q, k].astype(F32),
            )
            rows = (first_now / (jnp.sqrt(second_now) + EPSILON)).astype(BF16)
            for c in range(cols):
                piece[base + k * cols + c] = rows[:, c * LANES : (c + 1) * LANES]

        def start(unit, carry):
            @pl.when(unit != replica)
            def _():
                remote(
                    piece.at[unit],
                    gathered.at[replica],
                    swap_send.at[q, 2],
                    swap_recv.at[q, 2],
                    {"rep": unit},
                ).start()

            @pl.when(unit == replica)
            def _():
                gathered[unit] = piece[unit]

            return carry

        lax.fori_loop(base, base + units, start, 0)

    def unit_copy(q, count):
        return remote(
            gathered.at[pl.ds(0, count)],
            gathered.at[pl.ds(0, count)],
            swap_send.at[q, 2],
            swap_recv.at[q, 2],
            at_rep(1),
        )

    def row_copy(q, count):
        return remote(
            product.at[pl.ds(0, count)],
            product.at[pl.ds(0, count)],
            swap_send.at[q, 3],
            swap_recv.at[q, 3],
            at_rep(1),
        )

    def is_unit(q):
        return (replica >= q * units) & (replica < (q + 1) * units)

    def rotate_left(q):
        @pl.when(is_unit(q))
        def _():
            unit_copy(q, rep - 1).wait_recv()
            block = (replica - q * units) // cols
            back = jnp.dot(
                left[block],
                gathered[...].reshape(rep * 16, LANES),
                preferred_element_type=F32,
            )
            product[...] = back.astype(BF16).reshape(rep, 16, LANES)

            def start(step, carry):
                other = (replica + step) % rep
                remote(
                    product.at[other],
                    rows_in.at[replica],
                    swap_send.at[q, 3],
                    swap_recv.at[q, 3],
                    {"rep": other},
                ).start()
                return carry

            lax.fori_loop(1, rep, start, 0)
            rows_in[replica] = product[replica]

    def finish(q):
        @pl.when(is_unit(q))
        def _():
            row_copy(q, units - 1).wait_recv()

        @pl.when(jnp.logical_not(is_unit(q)))
        def _():
            row_copy(q, units).wait_recv()

        base = q * units
        for k in range(blocks):
            rows = jnp.concatenate([rows_in[base + k * cols + c] for c in range(cols)], axis=1)
            back = lax.dot_general(
                rows,
                right[k, :, q * width : (q + 1) * width],
                (((1,), (1,)), ((), ())),
                preferred_element_type=F32,
            )
            if q > 0:
                back = back + total_back[k]
            if q < chunks - 1:
                total_back[k] = back
            else:
                update[k] = back.astype(BF16)

    scope = jax.named_scope
    each = range(chunks)
    with scope("rotate_b"):
        rotate(half_blocks, blocks)
    with scope("greeting"):
        pl.semaphore_wait(barrier, fsdp + rep - 2)
    b = [sum_b(q) for q in each]
    for q in each:
        next(b[q])
    with scope("ranks"):
        ranks()
        load_first.wait()
        load_second.wait()
    with scope("to_shards0"):
        moments = [to_shards(0)]
    with scope("rotate_a"):
        rotate(0, half_blocks)
    a = [sum_a(q) for q in each]
    for q in each:
        next(a[q])
    turns = {}

    def go(*names):
        for name in names:
            turns[name] = turns.get(name, 1) + 1
            with scope(f"{name}_turn{turns[name]}"):
                next((a if name[0] == "a" else b)[int(name[1])], None)

    go("b0", "b1")
    for q in range(1, chunks):
        with scope(f"to_shards{q}"):
            moments.append(to_shards(q))
    go("a0", "b0", "a1", "b1")
    go("b0", "b1", "a0", "a1", "b0", "b1")
    with scope("lookups"):
        lookups()
    arrivals = []
    for q in each:
        go(f"a{q}", f"b{q}")
        if q < chunks - 1:
            with scope(f"to_owners{q}"):
                arrivals.append(to_owners(q))
        with scope(f"wait_moments{q}"):
            moments[q].wait_recv()
        with scope(f"to_units{q}"):
            to_units(q)
        if q == chunks - 1:
            with scope(f"to_owners{q}"):
                arrivals.append(to_owners(q))
    for q in each:
        with scope(f"rotate_left{q}"):
            rotate_left(q)
    for q in each:
        if q == chunks - 1:
            for earlier in each:
                with scope(f"finish{earlier}"):
                    finish(earlier)
        with scope(f"wait_owners{q}"):
            arrivals[q].wait_recv()
        with scope(f"keep_moments{q}"):
            keep_moments(q)

    with scope("sent"):
        for copy in sent:
            copy.wait_send()
    for q in each:

        @pl.when(is_unit(q))
        def _(q=q):
            unit_copy(q, units - 1).wait_send()
            row_copy(q, rep - 1).wait_send()

        @pl.when(jnp.logical_not(is_unit(q)))
        def _(q=q):
            unit_copy(q, units).wait_send()


def copy_kernel(*refs):
    count = len(refs) // 2
    sources, targets, sems = refs[:count], refs[count : 2 * count], refs[-1]
    copies = [
        pltpu.make_async_copy(source, target, sems.at[i])
        for i, (source, target) in enumerate(zip(sources, targets))
    ]
    for copy in copies:
        copy.start()
    for copy in copies:
        copy.wait()


def body(grad_partial, basis_left, basis_right, owner_table, moment_first, moment_second):
    fsdp = lax.axis_size("fsdp")
    rep = lax.axis_size("rep")
    blocks, size = basis_left.shape[0], basis_left.shape[1]
    slots, rows = moment_first.shape[1], moment_first.shape[2]
    nx = GRID_X
    ny = rep // nx
    width = size // CHUNKS
    half = blocks // 2
    cols = width // LANES
    sizes = (fsdp, nx, ny, CHUNKS, width, blocks, slots)
    anywhere = pl.BlockSpec(memory_space=pl.ANY)

    def vmem(*shape, kind=BF16):
        return pltpu.VMEM(shape, kind)

    tile = (rows, width)
    scratch = [
        vmem(blocks, size, size),
        vmem(blocks, size, size),
        vmem(blocks, size, size),
        vmem(slots, rows, size),
        vmem(slots, rows, size, kind=F32),
        vmem(blocks, rows, size, kind=F32),
        vmem(CHUNKS, nx, half, ny, *tile),
        vmem(CHUNKS, ny, blocks - half, nx, *tile),
        vmem(CHUNKS, 2, nx // 2, half, ny, *tile),
        vmem(CHUNKS, ny, half, *tile),
        vmem(CHUNKS, 2, ny // 2, blocks - half, nx, *tile),
        vmem(CHUNKS, nx, blocks - half, *tile),
        vmem(CHUNKS, blocks, *tile),
        [vmem(fsdp, *tile) for _ in range(CHUNKS)],
        [vmem(fsdp, *tile) for _ in range(CHUNKS)],
        [vmem(fsdp, 2, *tile) for _ in range(CHUNKS)],
        [vmem(fsdp, 2, *tile) for _ in range(CHUNKS)],
        vmem(CHUNKS * blocks * cols, rows, LANES),
        vmem(rep, rows, LANES),
        vmem(rep, rows, LANES),
        vmem(CHUNKS * blocks * cols, rows, LANES),
        pltpu.SMEM((2 * fsdp + slots + 1,), jnp.int32),
        pltpu.SemaphoreType.DMA((4, blocks)),
        pltpu.SemaphoreType.DMA((CHUNKS, 2, 2, ny // 2)),
        pltpu.SemaphoreType.DMA((CHUNKS, 2, 2, ny // 2)),
        pltpu.SemaphoreType.DMA((CHUNKS, 6)),
        pltpu.SemaphoreType.DMA((CHUNKS, 6)),
    ]
    results = pl.pallas_call(
        functools.partial(kernel, sizes),
        out_shape=(
            pltpu.VMEM((blocks, rows, size), BF16),
            pltpu.VMEM(moment_first.shape, BF16),
            pltpu.VMEM(moment_second.shape, F32),
        ),
        in_specs=[
            anywhere,
            anywhere,
            anywhere,
            pl.BlockSpec(memory_space=pltpu.SMEM),
            anywhere,
            anywhere,
        ],
        out_specs=(pl.BlockSpec(memory_space=pltpu.VMEM),) * 3,
        scratch_shapes=scratch,
        compiler_params=pltpu.CompilerParams(
            collective_id=0, has_side_effects=True, vmem_limit_bytes=56 * 1024 * 1024
        ),
    )(grad_partial, basis_left, basis_right, owner_table, moment_first, moment_second)
    return pl.pallas_call(
        copy_kernel,
        out_shape=tuple(jax.ShapeDtypeStruct(r.shape, r.dtype) for r in results),
        in_specs=[pl.BlockSpec(memory_space=pltpu.VMEM)] * 3,
        out_specs=(pl.BlockSpec(memory_space=pltpu.HBM),) * 3,
        scratch_shapes=[pltpu.SemaphoreType.DMA((3,))],
    )(*[pltpu.with_memory_space_constraint(r, pltpu.VMEM) for r in results])


def solution(mesh):
    placed = (
        P("rep", "fsdp", None, None),
        P("fsdp", None, None),
        P("fsdp", None, None),
        P(),
        P("fsdp", None, "rep", None),
        P("fsdp", None, "rep", None),
    )
    return jax.shard_map(
        body,
        mesh=mesh,
        in_specs=placed,
        out_specs=(
            P("fsdp", "rep", None),
            P("fsdp", None, "rep", None),
            P("fsdp", None, "rep", None),
        ),
        check_vma=False,
    )
```

```python
import functools

import jax
import jax.numpy as jnp
from jax import lax
from jax.experimental import pallas as pl
from jax.experimental.pallas import tpu as pltpu
from jax.sharding import PartitionSpec as P

BETA_ONE = 0.9
BETA_TWO = 0.95
EPSILON = 1e-08
GRID_X = 4
LANES = 128
CHUNKS = 2
F32 = jnp.float32
BF16 = jnp.bfloat16


def kernel(
    sizes,
    grad_hbm,
    left_hbm,
    right_hbm,
    table,
    first_hbm,
    second_hbm,
    update,
    new_first,
    new_second,
    grad,
    left,
    right,
    first,
    second,
    total_back,
    part_a,
    part_b,
    ring_a_x,
    direct_a,
    ring_b_y,
    direct_b,
    reduced,
    outgoing,
    incoming,
    sendback,
    comeback,
    piece,
    gathered,
    product,
    rows_in,
    slot_table,
    in_sem,
    ring_send,
    ring_recv,
    swap_send,
    swap_recv,
):
    fsdp, nx, ny, chunks, width, blocks, slots = sizes
    rep = nx * ny
    cols = width // LANES
    half_blocks = blocks // 2
    units = blocks * cols
    shard = lax.axis_index("fsdp")
    replica = lax.axis_index("rep")
    my_x = replica // ny
    my_y = replica % ny

    def wrap(value, count):
        return jnp.where(value >= count, value - count, value)

    def at_fsdp(step):
        return {"fsdp": wrap(shard + step, fsdp)}

    def at_rep(step):
        return {"rep": wrap(replica + step, rep)}

    def load(k, which):
        source, target = ((grad_hbm.at[0], grad), (left_hbm, left), (right_hbm, right))[which]
        return pltpu.make_async_copy(source.at[k], target.at[k], in_sem.at[which, k])

    def load_blocks(low, high):
        for k in range(low, high):
            for which in (0, 2, 1):
                load(k, which).start()

    load_blocks(half_blocks, blocks)
    barrier = pltpu.get_barrier_semaphore()

    def greet(axis):
        def body(step, carry):
            pl.semaphore_signal(
                barrier, inc=1, device_id=axis(step), device_id_type=pl.DeviceIdType.MESH
            )
            return carry

        return body

    lax.fori_loop(1, fsdp, greet(at_fsdp), 0, unroll=True)
    lax.fori_loop(1, rep, greet(at_rep), 0, unroll=True)
    load_first = pltpu.make_async_copy(first_hbm.at[0], first, in_sem.at[3, 0])
    load_second = pltpu.make_async_copy(second_hbm.at[0], second, in_sem.at[3, 1])
    load_first.start()
    load_second.start()

    def rotate(low, high):
        def body(k, carry):
            for which in (0, 2, 1):
                load(k, which).wait()
            right_part = jnp.dot(grad[k], right[k], preferred_element_type=F32)
            rotated = lax.dot_general(
                left[k],
                right_part.astype(BF16),
                (((0,), (0,)), ((), ())),
                preferred_element_type=F32,
            ).astype(BF16)
            for q in range(chunks):
                rows = rotated[:, q * width : (q + 1) * width].reshape(nx, ny, 16, width)
                if low == 0:
                    for x in range(nx):
                        part_a[q, x, k] = rows[x]
                else:
                    for y in range(ny):
                        part_b[q, y, k - low] = rows[:, y]
            return carry

        lax.fori_loop(low, high, body, 0)

    def remote(source, target, send, recv, device):
        return pltpu.make_async_remote_copy(
            src_ref=source,
            dst_ref=target,
            send_sem=send,
            recv_sem=recv,
            device_id=device,
            device_id_type=pl.DeviceIdType.MESH,
        )

    sent = []

    def ring(count, position, piece, landing, sems, device):
        reach = count // 2
        flying = {}

        def copy(way, step):
            there = (position + way * (reach - step + 1) + count) % count
            side = 0 if way > 0 else 1
            cut = None if step > 1 else side
            return remote(
                piece(there, cut),
                landing(side, step - 1, cut),
                ring_send.at[sems + (side, step - 1)],
                ring_recv.at[sems + (side, step - 1)],
                device(way),
            )

        for step in range(1, reach + 1):
            for way in (1, -1):
                side = 0 if way > 0 else 1
                if step > 1:
                    flying[way].wait_recv()
                    there = (position + way * (reach - step + 1) + count) % count
                    cut = side if step == 2 else None
                    held = piece(there, cut)
                    held[...] = held[...] + landing(side, step - 2, cut)[...]
                flying[way] = copy(way, step)
                flying[way].start()
                sent.append(flying[way])
            yield
        flying[1].wait_recv()
        flying[-1].wait_recv()

    def split(low, count, cut):
        if cut is None:
            return pl.ds(low, count)
        middle = (count + 1) // 2
        return pl.ds(low, middle) if cut == 0 else pl.ds(low + middle, count - middle)

    def along_x(way):
        return {"rep": ((my_x + way + nx) % nx) * ny + my_y}

    def along_y(way):
        return {"rep": my_x * ny + (my_y + way + ny) % ny}

    def total(own, landed):
        result = own.astype(F32)
        for value in landed:
            result = result + value.astype(F32)
        return result

    def direct(count, piece, landing, sems, device):
        for step in sorted(range(1, count), key=lambda step: -min(step, count - step)):
            remote(
                piece(step),
                landing.at[step],
                swap_send.at[sems],
                swap_recv.at[sems],
                device(step),
            ).start()
        others = landing.at[pl.ds(1, count - 1)]
        whole = remote(others, others, swap_send.at[sems], swap_recv.at[sems], device(1))
        sent.append(whole)
        return whole

    def sum_a(q):
        yield from ring(
            nx,
            my_x,
            lambda there, cut: part_a.at[q, there, :, split(0, ny, cut)],
            lambda side, step, cut: ring_a_x.at[q, side, step, :, split(0, ny, cut)],
            (q, 0),
            along_x,
        )
        for k in range(half_blocks):
            part_a[q, my_x, k] = total(
                part_a[q, my_x, k], [ring_a_x[q, side, nx // 2 - 1, k] for side in (0, 1)]
            ).astype(BF16)
        whole = direct(
            ny,
            lambda step: part_a.at[q, my_x, :, (my_y + step) % ny],
            direct_a.at[q],
            (q, 4),
            along_y,
        )
        yield
        whole.wait_recv()
        for k in range(half_blocks):
            reduced[q, k] = total(
                part_a[q, my_x, k, my_y], [direct_a[q, step, k] for step in range(1, ny)]
            ).astype(BF16)

    def sum_b(q):
        yield from ring(
            ny,
            my_y,
            lambda there, cut: part_b.at[q, there, :, split(0, nx, cut)],
            lambda side, step, cut: ring_b_y.at[q, side, step, :, split(0, nx, cut)],
            (q, 1),
            along_y,
        )
        for k in range(blocks - half_blocks):
            part_b[q, my_y, k] = total(
                part_b[q, my_y, k],
                [ring_b_y[q, side, ny // 2 - 1, k] for side in (0, 1)],
            ).astype(BF16)
        whole = direct(
            nx,
            lambda step: part_b.at[q, my_y, :, (my_x + step) % nx],
            direct_b.at[q],
            (q, 5),
            along_x,
        )
        yield
        whole.wait_recv()
        for k in range(blocks - half_blocks):
            reduced[q, half_blocks + k] = total(
                part_b[q, my_y, k, my_x],
                [direct_b[q, step, k] for step in range(1, nx)],
            ).astype(BF16)

    def ranks():
        def of_shard(other, rank):
            slot_table[other] = rank
            for k in range(blocks):
                rank += (table[other * blocks + k] == shard).astype(jnp.int32)
            return rank

        slot_table[2 * fsdp + slots] = lax.fori_loop(0, fsdp, of_shard, jnp.int32(0))

    def lookups():
        def of_shard(other, picks):
            rank = slot_table[other]
            away = (shard - other + fsdp) % fsdp
            return tuple(jnp.where(rank == j, away, picks[j]) for j in range(slots))

        picks = lax.fori_loop(0, fsdp, of_shard, (jnp.int32(0),) * slots)
        for j in range(slots):
            slot_table[2 * fsdp + j] = picks[j]

        def of_owner(owner, carry):
            block = jnp.int32(0)
            for k in range(blocks):
                block = jnp.where(table[shard * blocks + k] == owner, k, block)
            slot_table[fsdp + owner] = block
            return carry

        lax.fori_loop(0, fsdp, of_owner, 0)

    def swap(q, which, source, target, fill):
        def start(turn, carry):
            pair = turn // 2
            across = fsdp // 4 + jnp.where(pair % 2 == 0, pair // 2, -(pair + 1) // 2)
            step = 2 * across + 1 - turn % 2
            fill(source.at[step], wrap(shard + step, fsdp))
            remote(
                source.at[step],
                target.at[step],
                swap_send.at[q, which],
                swap_recv.at[q, which],
                at_fsdp(step),
            ).start()
            return carry

        lax.fori_loop(0, fsdp - 1, start, 0, unroll=True)
        fill(target.at[0], shard)
        others = pl.ds(1, fsdp - 1)
        whole = remote(
            source.at[others],
            target.at[others],
            swap_send.at[q, which],
            swap_recv.at[q, which],
            at_fsdp(1),
        )
        sent.append(whole)
        return whole

    def to_owners(q):
        def fill(slot, owner):
            slot[...] = reduced[q, slot_table[fsdp + owner]]

        return swap(q, 0, outgoing[q], incoming[q], fill)

    def to_shards(q):
        columns = pl.ds(q * width, width)

        def fill(slot, other):
            held = jnp.minimum(slot_table[other], slots - 1)
            slot[0] = first[held, :, columns]
            slot[1] = second[held, :, columns].astype(BF16)

        return swap(q, 1, sendback[q], comeback[q], fill)

    def advanced(first_old, second_old, gradient):
        first_now = BETA_ONE * first_old + (1.0 - BETA_ONE) * gradient
        second_now = BETA_TWO * second_old + (1.0 - BETA_TWO) * gradient * gradient
        return first_now, second_now

    def keep_moments(q):
        columns = pl.ds(q * width, width)
        count = slot_table[2 * fsdp + slots]

        def body(j, carry):
            gradient = incoming[q][slot_table[2 * fsdp + j]].astype(F32)
            first_old = first[j, :, columns].astype(F32)
            second_old = second[j, :, columns]
            first_now, second_now = advanced(first_old, second_old, gradient)
            used = j < count
            new_first[0, j, :, columns] = jnp.where(used, first_now, first_old).astype(BF16)
            new_second[0, j, :, columns] = jnp.where(used, second_now, second_old)
            return carry

        lax.fori_loop(0, slots, body, 0)

    def to_units(q):
        base = q * units

        for k in range(blocks):
            away = (shard - table[shard * blocks + k] + fsdp) % fsdp
            first_now, second_now = advanced(
                comeback[q][away, 0].astype(F32),
                comeback[q][away, 1].astype(F32),
                reduced[q, k].astype(F32),
            )
            rows = (first_now / (jnp.sqrt(second_now) + EPSILON)).astype(BF16)
            for c in range(cols):
                piece[base + k * cols + c] = rows[:, c * LANES : (c + 1) * LANES]

        def start(unit, carry):
            @pl.when(unit != replica)
            def _():
                remote(
                    piece.at[unit],
                    gathered.at[replica],
                    swap_send.at[q, 2],
                    swap_recv.at[q, 2],
                    {"rep": unit},
                ).start()

            @pl.when(unit == replica)
            def _():
                gathered[unit] = piece[unit]

            return carry

        lax.fori_loop(base, base + units, start, 0)

    def unit_copy(q, count):
        return remote(
            gathered.at[pl.ds(0, count)],
            gathered.at[pl.ds(0, count)],
            swap_send.at[q, 2],
            swap_recv.at[q, 2],
            at_rep(1),
        )

    def row_copy(q, count):
        return remote(
            product.at[pl.ds(0, count)],
            product.at[pl.ds(0, count)],
            swap_send.at[q, 3],
            swap_recv.at[q, 3],
            at_rep(1),
        )

    def is_unit(q):
        return (replica >= q * units) & (replica < (q + 1) * units)

    def rotate_left(q):
        @pl.when(is_unit(q))
        def _():
            unit_copy(q, rep - 1).wait_recv()
            block = (replica - q * units) // cols
            back = jnp.dot(
                left[block],
                gathered[...].reshape(rep * 16, LANES),
                preferred_element_type=F32,
            )
            product[...] = back.astype(BF16).reshape(rep, 16, LANES)

            def start(step, carry):
                other = wrap(replica + step, rep)
                remote(
                    product.at[other],
                    rows_in.at[replica],
                    swap_send.at[q, 3],
                    swap_recv.at[q, 3],
                    {"rep": other},
                ).start()
                return carry

            lax.fori_loop(1, rep, start, 0)
            rows_in[replica] = product[replica]

    def finish(q):
        @pl.when(is_unit(q))
        def _():
            row_copy(q, units - 1).wait_recv()

        @pl.when(jnp.logical_not(is_unit(q)))
        def _():
            row_copy(q, units).wait_recv()

        base = q * units
        for k in range(blocks):
            rows = jnp.concatenate([rows_in[base + k * cols + c] for c in range(cols)], axis=1)
            back = lax.dot_general(
                rows,
                right[k, :, q * width : (q + 1) * width],
                (((1,), (1,)), ((), ())),
                preferred_element_type=F32,
            )
            if q > 0:
                back = back + total_back[k]
            if q < chunks - 1:
                total_back[k] = back
            else:
                update[k] = back.astype(BF16)

    scope = jax.named_scope
    each = range(chunks)
    with scope("rotate_b"):
        rotate(half_blocks, blocks)
    with scope("greeting"):
        pl.semaphore_wait(barrier, fsdp + rep - 2)
    b = [sum_b(q) for q in each]
    for q in each:
        next(b[q])
    load_blocks(0, half_blocks)
    with scope("ranks"):
        ranks()
        load_first.wait()
        load_second.wait()
    with scope("to_shards0"):
        moments = [to_shards(0)]
    with scope("rotate_a"):
        rotate(0, half_blocks)
    a = [sum_a(q) for q in each]
    for q in each:
        next(a[q])
    turns = {}

    def go(*names):
        for name in names:
            turns[name] = turns.get(name, 1) + 1
            with scope(f"{name}_turn{turns[name]}"):
                next((a if name[0] == "a" else b)[int(name[1])], None)

    go("b0", "b1")
    for q in range(1, chunks):
        with scope(f"to_shards{q}"):
            moments.append(to_shards(q))
    go("a0", "b0", "a1", "b1")
    go("b0", "b1", "a0", "a1", "b0", "b1")
    with scope("lookups"):
        lookups()
    arrivals = []
    for q in each:
        go(f"a{q}", f"b{q}")
        if q < chunks - 1:
            with scope(f"to_owners{q}"):
                arrivals.append(to_owners(q))
        with scope(f"wait_moments{q}"):
            moments[q].wait_recv()
        with scope(f"to_units{q}"):
            to_units(q)
        if q == chunks - 1:
            with scope(f"to_owners{q}"):
                arrivals.append(to_owners(q))
    for q in each:
        with scope(f"rotate_left{q}"):
            rotate_left(q)
    for q in each:
        if q == chunks - 1:
            for earlier in each:
                with scope(f"finish{earlier}"):
                    finish(earlier)
        with scope(f"wait_owners{q}"):
            arrivals[q].wait_recv()
        with scope(f"keep_moments{q}"):
            keep_moments(q)

    with scope("sent"):
        for copy in sent:
            copy.wait_send()
    for q in each:

        @pl.when(is_unit(q))
        def _(q=q):
            unit_copy(q, units - 1).wait_send()
            row_copy(q, rep - 1).wait_send()

        @pl.when(jnp.logical_not(is_unit(q)))
        def _(q=q):
            unit_copy(q, units).wait_send()


def copy_kernel(*refs):
    count = len(refs) // 2
    sources, targets, sems = refs[:count], refs[count : 2 * count], refs[-1]
    copies = [
        pltpu.make_async_copy(source, target, sems.at[i])
        for i, (source, target) in enumerate(zip(sources, targets))
    ]
    for copy in copies:
        copy.start()
    for copy in copies:
        copy.wait()


def body(grad_partial, basis_left, basis_right, owner_table, moment_first, moment_second):
    fsdp = lax.axis_size("fsdp")
    rep = lax.axis_size("rep")
    blocks, size = basis_left.shape[0], basis_left.shape[1]
    slots, rows = moment_first.shape[1], moment_first.shape[2]
    nx = GRID_X
    ny = rep // nx
    width = size // CHUNKS
    half = blocks // 2
    cols = width // LANES
    sizes = (fsdp, nx, ny, CHUNKS, width, blocks, slots)
    anywhere = pl.BlockSpec(memory_space=pl.ANY)

    def vmem(*shape, kind=BF16):
        return pltpu.VMEM(shape, kind)

    tile = (rows, width)
    scratch = [
        vmem(blocks, size, size),
        vmem(blocks, size, size),
        vmem(blocks, size, size),
        vmem(slots, rows, size),
        vmem(slots, rows, size, kind=F32),
        vmem(blocks, rows, size, kind=F32),
        vmem(CHUNKS, nx, half, ny, *tile),
        vmem(CHUNKS, ny, blocks - half, nx, *tile),
        vmem(CHUNKS, 2, nx // 2, half, ny, *tile),
        vmem(CHUNKS, ny, half, *tile),
        vmem(CHUNKS, 2, ny // 2, blocks - half, nx, *tile),
        vmem(CHUNKS, nx, blocks - half, *tile),
        vmem(CHUNKS, blocks, *tile),
        [vmem(fsdp, *tile) for _ in range(CHUNKS)],
        [vmem(fsdp, *tile) for _ in range(CHUNKS)],
        [vmem(fsdp, 2, *tile) for _ in range(CHUNKS)],
        [vmem(fsdp, 2, *tile) for _ in range(CHUNKS)],
        vmem(CHUNKS * blocks * cols, rows, LANES),
        vmem(rep, rows, LANES),
        vmem(rep, rows, LANES),
        vmem(CHUNKS * blocks * cols, rows, LANES),
        pltpu.SMEM((2 * fsdp + slots + 1,), jnp.int32),
        pltpu.SemaphoreType.DMA((4, blocks)),
        pltpu.SemaphoreType.DMA((CHUNKS, 2, 2, ny // 2)),
        pltpu.SemaphoreType.DMA((CHUNKS, 2, 2, ny // 2)),
        pltpu.SemaphoreType.DMA((CHUNKS, 6)),
        pltpu.SemaphoreType.DMA((CHUNKS, 6)),
    ]
    results = pl.pallas_call(
        functools.partial(kernel, sizes),
        out_shape=(
            pltpu.VMEM((blocks, rows, size), BF16),
            pltpu.VMEM(moment_first.shape, BF16),
            pltpu.VMEM(moment_second.shape, F32),
        ),
        in_specs=[
            anywhere,
            anywhere,
            anywhere,
            pl.BlockSpec(memory_space=pltpu.SMEM),
            anywhere,
            anywhere,
        ],
        out_specs=(pl.BlockSpec(memory_space=pltpu.VMEM),) * 3,
        scratch_shapes=scratch,
        compiler_params=pltpu.CompilerParams(
            collective_id=0, has_side_effects=True, vmem_limit_bytes=56 * 1024 * 1024
        ),
    )(grad_partial, basis_left, basis_right, owner_table, moment_first, moment_second)
    return pl.pallas_call(
        copy_kernel,
        out_shape=tuple(jax.ShapeDtypeStruct(r.shape, r.dtype) for r in results),
        in_specs=[pl.BlockSpec(memory_space=pltpu.VMEM)] * 3,
        out_specs=(pl.BlockSpec(memory_space=pltpu.HBM),) * 3,
        scratch_shapes=[pltpu.SemaphoreType.DMA((3,))],
    )(*[pltpu.with_memory_space_constraint(r, pltpu.VMEM) for r in results])


def solution(mesh):
    placed = (
        P("rep", "fsdp", None, None),
        P("fsdp", None, None),
        P("fsdp", None, None),
        P(),
        P("fsdp", None, "rep", None),
        P("fsdp", None, "rep", None),
    )
    return jax.shard_map(
        body,
        mesh=mesh,
        in_specs=placed,
        out_specs=(
            P("fsdp", "rep", None),
            P("fsdp", None, "rep", None),
            P("fsdp", None, "rep", None),
        ),
        check_vma=False,
    )
```
